512 devices in a mesh: grp: 16 (over y, x), wide: 32 (over z, core).
Axes of the slice: x: 4, y: 4, z: 16, core: 2. Of those that a mesh axis runs over, the one named last changes fastest.
Arguments:
- null_space: bfloat16 [16, 4096, 1152], P('grp', 'wide'), may hold values from -6 to 6
- node_damage: int32 [16, 4096, 64], P('grp', 'wide'), may hold values from 0 to 7
- face_target: int32 [16, 4096, 3], P('grp', 'wide'), may hold values from 0 to 191
- face_damage: int32 [16, 4096, 3], P('grp', 'wide'), may hold values from 0 to 7
- ghost_lists: int32 [16, 32, 4, 16], P('grp', 'wide'), may hold values from 0 to 127
- agg_owner: int32 [16, 4096, 1], P('grp', 'wide'), may hold values from 0 to 31; in each aligned block of 128 rows (0 to 127, 128 to 255, ..., all dimensions but the last counted through in order) at most 8 rows name the same one
- stiffness: bfloat16 [192, 768], replicated, as said below
Outputs:
- coarse_rows: float32 [16, 4608, 256], P('grp', 'wide')
The draws below stay inside these ranges and needn't reach their ends.
Inputs may be any that keep to these rules, and one draw needn't show every extreme that they name: `agg_owner`: no more than 8 aggregates of one device share an owner, and exactly that many do on some device. `stiffness`: each 192 x 192 block is symmetric.
All inputs are finite; a program needn't handle non-finite values.
Results may differ from the reference program's by a relative error of at most 0.0027.
Values may be sent and summed in bfloat16 or wider, within the bound.
A program may use at most 64 MiB of HBM per device.

```python
import math
import jax
import jax.numpy as jnp
import numpy as np
from jax import lax

AGG_DEV = 128
NODES_AGG = 64
MODES = 6
FACES = 3
LEVELS = 8
DOFS = 192
GHOST = 16
SEND_CAP = 8
ROW = 144
N_GRP = 16
N_WIDE = 32


def symmetric(random_part, diagonal_part):
    swapped = jnp.swapaxes(random_part, -1, -2)
    eye_part = jnp.eye(DOFS, dtype=jnp.float32)
    return (random_part + swapped) * (0.70710678 / DOFS) + eye_part * diagonal_part[..., None] / DOFS


def draw_stiffness(key, part):
    key = jax.random.fold_in(key, 11)
    key_entries, key_diagonal = jax.random.split(key)
    random_part = jax.random.normal(key_entries, (1 + FACES, DOFS, DOFS), jnp.float32)
    diagonal_part = jax.random.uniform(key_diagonal, (1 + FACES, DOFS), jnp.float32, 1.0, 3.0)
    blocks = symmetric(random_part, diagonal_part)
    side_by_side = jnp.transpose(blocks, (1, 0, 2)).reshape(DOFS, (1 + FACES) * DOFS)
    return side_by_side.astype(jnp.bfloat16)


def plant(result, own_key, least, high):
    extent = result.shape
    index_at = [jax.random.randint(jax.random.fold_in(own_key, axis), (), 0, extent[axis]) for axis in range(len(extent))]
    result = result.at[tuple(index_at)].set(least)
    longest = extent.index(max(extent))
    index_at[longest] = (index_at[longest] + 1) % extent[longest]
    return result.at[tuple(index_at)].set(high)


def level_of(rng, extent, cuts, low, high):
    def one(dim, parts):
        draws = jax.random.uniform(jax.random.fold_in(jax.random.fold_in(rng, 6), dim), (parts,), jnp.float32, low / len(cuts), high / len(cuts))
        return jnp.repeat(jnp.exp(draws), extent[dim] // parts).reshape((-1,) + (1,) * (len(extent) - dim - 1))

    level = one(*cuts[0])
    for cut in cuts[1:]:
        level = level * one(*cut)
    return level


def deal_out(stream_key, own, number, rows, amount, top, bound, slope):
    sequence = jax.random.permutation(stream_key, amount)
    packed, ordinary = portions_of(amount, rows * top, bound, slope, True), portions_of(amount, rows * top, bound, slope, False)
    places = jnp.arange(amount)

    def named(tallies, rotation):
        used = int((tallies > 0).sum())
        fixed = max(1, used // 4)
        passed = fixed + (places - fixed + rotation * (used - fixed)) % max(1, amount - fixed)
        return jnp.zeros((amount,), jnp.int32).at[sequence[jnp.where(places < fixed, places, passed)]].set(jnp.asarray(tallies, jnp.int32))

    tallies = jnp.where(number % 4 == 0, named(packed, number // 4), named(ordinary, number - number // 4 - 1))
    mixed = jax.random.permutation(jax.random.fold_in(own, 3), amount)
    donor, taker = mixed[0:amount // 2 * 2:2], mixed[1:amount // 2 * 2:2]
    room = jnp.minimum(tallies[donor] - 1, bound - tallies[taker]) // 2
    room = jnp.where((donor == sequence[0]) | (taker == sequence[0]) | (tallies[taker] == 0), 0, jnp.maximum(room, 0))
    passed = jax.random.randint(jax.random.fold_in(own, 4), (amount // 2,), 0, 1 << 20) % (room + 1)
    tallies = tallies.at[donor].add(-passed).at[taker].add(passed)
    labels = jnp.searchsorted(jnp.cumsum(tallies), jnp.arange(rows * top), side="right").astype(jnp.int32)
    table = labels.reshape(top, rows).T
    table = table[jax.random.permutation(jax.random.fold_in(own, 1), rows)]
    rotation = jax.random.randint(jax.random.fold_in(own, 2), (rows, 1), 0, top)
    return jnp.take_along_axis(table, (jnp.arange(top)[None, :] + rotation) % top, axis=1)


def portions_of(count, total, most, skew, full):
    weights = [(1 << 20) // math.isqrt(rank ** skew) + 1 for rank in range(1, count + 1)]
    largest = most if full else min(most, max(-(-total // count), total * weights[0] // sum(weights)))
    least = 1 if total - largest >= count - 1 else 0
    counts, spare = [largest] + [least] * (count - 1), total - largest - least * (count - 1)
    while spare > 0:
        movable = [i for i in range(1, count) if counts[i] < largest] or [i for i in range(1, count) if counts[i] < most]
        whole, left = sum([weights[i] for i in movable]), spare
        for i in movable:
            more = min(most - counts[i], max(1, left * weights[i] // whole), spare)
            counts[i] = counts[i] + more
            spare = spare - more
    return np.array(counts)


def noise(own_key, dims, deviation, most, pieces=(), kind=jnp.bfloat16):
    array = deviation * jax.random.normal(own_key, dims, jnp.float32)
    if pieces:
        array = array * level_of(own_key, dims, pieces, -0.22, 0.18)
    return jnp.clip(array, -most, most).astype(kind)


def setup_inputs(seed: int = 0) -> dict:
    key_list = jax.random.split(jax.random.key(seed), 8)
    null_space = noise(key_list[0], (N_GRP, N_WIDE * AGG_DEV, MODES * DOFS), 1.0, 6.0, ((0, 16), (1, 32)))
    node_damage = plant(jax.random.randint(key_list[1], (N_GRP, N_WIDE * AGG_DEV, NODES_AGG), 0, LEVELS), jax.random.fold_in(key_list[1], 1), 0, LEVELS - 1).astype(jnp.int32)
    face_target = plant(jax.random.randint(key_list[2], (N_GRP, N_WIDE * AGG_DEV, FACES), 0, AGG_DEV + 4 * GHOST), jax.random.fold_in(key_list[2], 1), 0, (AGG_DEV + 4 * GHOST) - 1).astype(jnp.int32)
    face_damage = plant(jax.random.randint(key_list[3], (N_GRP, N_WIDE * AGG_DEV, FACES), 0, LEVELS), jax.random.fold_in(key_list[3], 1), 0, LEVELS - 1).astype(jnp.int32)
    ghost_lists = plant(jax.random.randint(key_list[4], (N_GRP, N_WIDE, 4, GHOST), 0, AGG_DEV), jax.random.fold_in(key_list[4], 1), 0, AGG_DEV - 1).astype(jnp.int32)
    agg_owner_keys = jax.random.split(jax.random.fold_in(key_list[5], 1), N_GRP * (N_WIDE * AGG_DEV) // AGG_DEV)
    agg_owner_turns = jax.random.permutation(jax.random.fold_in(key_list[5], 3), N_GRP * (N_WIDE * AGG_DEV) // AGG_DEV)
    agg_owner = jax.vmap(lambda own, number: deal_out(jax.random.fold_in(key_list[5], 2), own, number, AGG_DEV, N_WIDE, 1, SEND_CAP, 1))(agg_owner_keys, agg_owner_turns).reshape((N_GRP, N_WIDE * AGG_DEV, 1))
    stiffness = draw_stiffness(jax.random.fold_in(key_list[7], 71), 0)
    return {"null_space": null_space, "node_damage": node_damage, "face_target": face_target, "face_damage": face_damage, "ghost_lists": ghost_lists, "agg_owner": agg_owner, "stiffness": stiffness}


def shift_down(values, axis):
    length = values.shape[axis]
    zero_part = jnp.zeros_like(lax.slice_in_dim(values, 0, 1, axis=axis))
    return jnp.concatenate([zero_part, lax.slice_in_dim(values, 0, length - 1, axis=axis)], axis=axis)


def shift_up(values, axis):
    length = values.shape[axis]
    zero_part = jnp.zeros_like(lax.slice_in_dim(values, 0, 1, axis=axis))
    return jnp.concatenate([lax.slice_in_dim(values, 1, length, axis=axis), zero_part], axis=axis)


def weighted_modes(inputs):
    null_part, damage_part = inputs
    null_part = null_part.reshape(null_part.shape[0], MODES, DOFS)
    scales = (LEVELS - damage_part).astype(jnp.float32) / LEVELS
    scales = jnp.repeat(scales, 3, axis=-1)
    return (null_part.astype(jnp.float32) * scales[..., None, :]).astype(jnp.bfloat16)


def project(left, matrix):
    return jnp.einsum('amd,de->ame', left.astype(jnp.float32), matrix.astype(jnp.float32)).astype(jnp.bfloat16)


def paired(left, right):
    return jnp.einsum('amd,and->amn', left.astype(jnp.float32), right.astype(jnp.float32))


def reference(null_space, node_damage, face_target, face_damage, ghost_lists, agg_owner, stiffness):
    interior_stiff = stiffness[:, :DOFS]
    weighted = lax.map(weighted_modes, (null_space, node_damage))
    grouped = weighted.reshape(N_GRP, N_WIDE, AGG_DEV, MODES, DOFS)
    picked = jax.vmap(jax.vmap(lambda source, listed: source[listed]))(grouped, ghost_lists)
    from_grp_lower = shift_down(picked[:, :, 1], 0)
    from_grp_upper = shift_up(picked[:, :, 0], 0)
    from_wide_lower = shift_down(picked[:, :, 3], 1)
    from_wide_upper = shift_up(picked[:, :, 2], 1)
    ghosts = jnp.stack([from_grp_lower, from_grp_upper, from_wide_lower, from_wide_upper], axis=2)
    span = AGG_DEV + 4 * GHOST

    def local_group(inputs):
        modes, ghost_in, targets, damage = inputs
        targets = targets.reshape(N_WIDE, AGG_DEV, FACES)
        damage = damage.reshape(N_WIDE * AGG_DEV, FACES)
        lookup = jnp.concatenate([modes, ghost_in.reshape(N_WIDE, 4 * GHOST, MODES, DOFS)], axis=1)
        flat_modes = modes.reshape(N_WIDE * AGG_DEV, MODES, DOFS)
        diag = paired(project(flat_modes, interior_stiff), flat_modes)
        face_blocks = []
        contribs = []
        indices = []
        for index in range(FACES):
            face_matrix = stiffness[:, (index + 1) * DOFS:(index + 2) * DOFS]
            other = jax.vmap(lambda source, picks: source[picks])(lookup, targets[:, :, index])
            other = other.reshape(N_WIDE * AGG_DEV, MODES, DOFS)
            level = (LEVELS - damage[:, index]).astype(jnp.float32) / LEVELS
            weight = (level * level)[:, None, None]
            near = project(flat_modes, face_matrix)
            far = project(other, face_matrix)
            diag = diag + weight * paired(near, flat_modes)
            face_blocks.append(-weight * paired(near, other))
            contribs.append(weight * paired(far, other))
            indices.append((jnp.arange(N_WIDE, dtype=jnp.int32)[:, None] * span + targets[:, :, index]).reshape(-1))
        values = jnp.stack(contribs).reshape(FACES * N_WIDE * AGG_DEV, MODES * MODES)
        buckets = jax.ops.segment_sum(values, jnp.concatenate(indices), num_segments=N_WIDE * span)
        buckets = buckets.reshape(N_WIDE, span, MODES * MODES)
        diag_total = diag.reshape(N_WIDE, AGG_DEV, MODES * MODES) + buckets[:, :AGG_DEV]
        returns = buckets[:, AGG_DEV:].reshape(N_WIDE, 4, GHOST, MODES * MODES)
        faces = jnp.stack(face_blocks, axis=1).reshape(N_WIDE, AGG_DEV, FACES * MODES * MODES)
        return diag_total, faces, returns

    diag_total, faces, returns = lax.map(local_group, (grouped, ghosts, face_target, face_damage))
    incoming = jnp.stack([shift_down(returns[:, :, 1], 0), shift_up(returns[:, :, 0], 0),
                          shift_down(returns[:, :, 3], 1), shift_up(returns[:, :, 2], 1)], axis=2)
    device_base = (jnp.arange(N_GRP, dtype=jnp.int32)[:, None] * N_WIDE + jnp.arange(N_WIDE, dtype=jnp.int32)[None, :]) * AGG_DEV
    list_index = (device_base[:, :, None, None] + ghost_lists).reshape(-1)
    added = jax.ops.segment_sum(incoming.reshape(-1, MODES * MODES), list_index, num_segments=N_GRP * N_WIDE * AGG_DEV)
    diag_total = diag_total + added.reshape(N_GRP, N_WIDE, AGG_DEV, MODES * MODES)
    coarse = jnp.concatenate([diag_total, faces], axis=-1)
    owners = agg_owner.reshape(N_GRP, N_WIDE, AGG_DEV)
    onehot = (owners[..., None] == jnp.arange(N_WIDE, dtype=jnp.int32)).astype(jnp.int32)
    ranks = jnp.sum((jnp.cumsum(onehot, axis=2) - onehot) * onehot, axis=-1)
    group_index = jnp.arange(N_GRP, dtype=jnp.int32)[:, None, None]
    wide_index = jnp.arange(N_WIDE, dtype=jnp.int32)[None, :, None]
    flat_slot = ((group_index * N_WIDE + owners) * N_WIDE + wide_index) * SEND_CAP + ranks
    placed = jnp.zeros((N_GRP * N_WIDE * N_WIDE * SEND_CAP, ROW), jnp.float32)
    placed = placed.at[flat_slot.reshape(-1)].set(coarse.reshape(-1, ROW))
    placed = placed.reshape(N_GRP, N_WIDE, N_WIDE * SEND_CAP, ROW)
    placed = jnp.transpose(placed, (0, 1, 3, 2))
    return placed.reshape(N_GRP, N_WIDE * ROW, N_WIDE * SEND_CAP)
```

```python
import functools

import jax
import jax.numpy as jnp
from jax import lax
from jax.experimental import pallas as pl
from jax.experimental.pallas import tpu as pltpu
from jax.sharding import PartitionSpec as P

AGG = 128
MODES = 6
DOFS = 192
FACES = 3
LEVELS = 8
GHOST = 16
CAP = 8
WIDTH = MODES * DOFS
BLOCK = MODES * MODES
ROW = (1 + FACES) * BLOCK
MESSAGE = WIDTH + 128
MESH = pl.DeviceIdType.MESH
F32 = jnp.float32
BF16 = jnp.bfloat16


def lanes_dot(left, right):
    return lax.dot_general(left, right, (((1,), (1,)), ((), ())), preferred_element_type=F32)


def plain_dot(left, right):
    return jnp.dot(left, right, preferred_element_type=F32)


def ones_where(condition):
    return jnp.where(condition, 1.0, 0.0).astype(BF16)


def iota(shape, dim):
    return lax.broadcasted_iota(jnp.int32, shape, dim)


def pair_sums(load_left, load_right):
    def step(i, sums):
        base = pl.multiple_of(i * 16, 16)
        left = [load_left(m, base).astype(F32) for m in range(MODES)]
        right = [load_right(n, base).astype(F32) for n in range(MODES)]
        new = []
        for m in range(MODES):
            for n in range(MODES):
                product = left[m] * right[n]
                new.append(sums[m * MODES + n] + (product[:8] + product[8:]))
        return tuple(new)

    zero = jnp.zeros((8, AGG), F32)
    return lax.fori_loop(0, DOFS // 16, step, (zero,) * BLOCK)


def kernel(
    grp_size, wide_size,
    null_hbm, damage_hbm, target_hbm, face_hbm, list_hbm, owner_hbm, stiff_hbm,
    out_ref,
    null_v, damage_v, target_v, face_v, list_v, owner_v, stiff_v,
    message_out, message_in, modes_t, stiff_t, near_s, other_s, partial_s, sums_s, place_s, send_s, recv_s,
    in_sem, ghost_send, ghost_recv, row_send, row_recv,
):
    g = lax.axis_index("grp")
    w = lax.axis_index("wide")

    loads = [
        pltpu.make_async_copy(source, target, in_sem.at[k])
        for k, (source, target) in enumerate(
            [
                (list_hbm, list_v), (damage_hbm, damage_v), (null_hbm, null_v), (target_hbm, target_v),
                (face_hbm, face_v), (owner_hbm, owner_v), (stiff_hbm, stiff_v),
            ]
        )
    ]
    for load in loads:
        load.start()

    barrier = pltpu.get_barrier_semaphore()

    def greet(k, carry):
        pl.semaphore_signal(barrier, inc=1, device_id=(g, lax.rem(w + k, wide_size)), device_id_type=MESH)
        return carry

    lax.fori_loop(1, wide_size, greet, 0)
    grp_lower = lax.rem(g + grp_size - 1, grp_size)
    grp_upper = lax.rem(g + 1, grp_size)
    for neighbour in (grp_lower, grp_upper):
        pl.semaphore_signal(barrier, inc=1, device_id=(neighbour, w), device_id_type=MESH)

    loads[0].wait()
    listed = list_v[...].astype(F32)
    spread = jnp.concatenate([jnp.broadcast_to(listed[r : r + 1], (GHOST, GHOST)) for r in range(4)], axis=0)
    on_diagonal = (iota((4 * GHOST, GHOST), 0) & (GHOST - 1)) == iota((4 * GHOST, GHOST), 1)
    list_column = jnp.sum(jnp.where(on_diagonal, spread, 0.0), axis=1, keepdims=True).astype(jnp.int32)
    select = ones_where(list_column == iota((4 * GHOST, AGG), 1))

    loads[1].wait()
    levels = ((LEVELS - damage_v[...]).astype(F32) * (1.0 / LEVELS)).T.astype(BF16)
    node_of = ((iota((1, WIDTH), 1) * 43691) >> 17) & 63
    widen = ones_where(iota((64, WIDTH), 0) == node_of)
    scales = plain_dot(levels, widen)
    loads[2].wait()
    modes = (null_v[...].astype(F32) * scales).astype(BF16)
    picked = plain_dot(select, modes).astype(BF16)

    loads[3].wait()
    loads[4].wait()
    targets = jnp.concatenate([target_v[f] for f in range(FACES)], axis=1)
    levels_f = jnp.concatenate([face_v[f] for f in range(FACES)], axis=1)
    level = (LEVELS - levels_f).astype(F32) * (1.0 / LEVELS)
    weight = level * level
    chosen = ones_where(iota((AGG + 4 * GHOST, FACES * AGG), 0) == targets)
    row = iota((AGG, FACES * AGG), 0)
    face_of = iota((AGG, FACES * AGG), 1) >> 7
    weight_rows = jnp.where((row == face_of) | (row == face_of + FACES), weight, 0.0).astype(BF16)
    weight_local = lanes_dot(weight_rows[:16], chosen[:AGG])
    weight_ghost = lanes_dot(chosen[AGG:], weight_rows)
    high = weight_ghost.astype(BF16).astype(F32)
    split = jnp.where(iota((4 * GHOST, 128), 1) < FACES, high, weight_ghost - high).astype(BF16)
    for r in range(4):
        message_out[r, :, :WIDTH] = picked[r * GHOST : (r + 1) * GHOST]
        message_out[r, :, WIDTH:] = split[r * GHOST : (r + 1) * GHOST]

    pl.semaphore_wait(barrier, wide_size + 1)
    wide_lower = lax.rem(w + wide_size - 1, wide_size)
    wide_upper = lax.rem(w + 1, wide_size)
    ghost_copies = [
        pltpu.make_async_remote_copy(
            src_ref=message_out.at[r],
            dst_ref=message_in.at[r ^ 1],
            send_sem=ghost_send.at[r],
            recv_sem=ghost_recv.at[r ^ 1],
            device_id=peer,
            device_id_type=MESH,
        )
        for r, peer in enumerate([(grp_lower, w), (grp_upper, w), (g, wide_lower), (g, wide_upper)])
    ]
    for copy in ghost_copies:
        copy.start()

    modes_t[...] = modes.T
    loads[6].wait()
    stiff_t[...] = stiff_v[...].T
    for pair in range(MODES // 2):
        two = jnp.concatenate(
            [modes_t[(2 * pair + h) * DOFS : (2 * pair + h + 1) * DOFS] for h in range(2)], axis=1
        )
        product = plain_dot(stiff_t[...], two).astype(BF16)
        near_s[2 * pair] = product[:, :AGG]
        near_s[2 * pair + 1] = product[:, AGG:]

    loads[5].wait()
    owner = owner_v[0]
    owned = iota((wide_size, AGG), 0) == owner
    before = ones_where(iota((AGG, AGG), 0) < iota((AGG, AGG), 1))
    earlier = plain_dot(ones_where(owned), before)
    rank = jnp.sum(jnp.where(owned, earlier, 0.0), axis=0, keepdims=True).astype(jnp.int32)
    place_s[...] = ones_where(iota((wide_size * CAP, AGG), 0) == owner * CAP + rank)

    def load_modes(m, base):
        return modes_t[pl.ds(m * DOFS + base, 16), :]

    for k in range(1 + FACES):
        sums = pair_sums(lambda m, base, k=k: near_s[m, pl.ds(k * DOFS + base, 16), :], load_modes)
        for entry in range(BLOCK):
            partial_s[k, entry * 8 : entry * 8 + 8] = sums[entry]

    for copy in ghost_copies:
        copy.wait_recv()
    valid = [g > 0, g < grp_size - 1, w > 0, w < wide_size - 1]
    arrived = jnp.concatenate(
        [jnp.where(valid[r], message_in[r].astype(F32), 0.0) for r in range(4)], axis=0
    ).astype(BF16)
    arrived_t = arrived.T
    ghosts_t = arrived_t[:WIDTH]
    weight_back = plain_dot(arrived_t[WIDTH : WIDTH + 16], select)
    for f in range(FACES):
        at = slice(f * AGG, (f + 1) * AGG)
        other = plain_dot(modes_t[...], chosen[:AGG, at]) + plain_dot(ghosts_t, chosen[AGG:, at])
        other_s[f] = other.astype(BF16)

    total = []
    for f in range(FACES):
        total.append(
            weight[:, f * AGG : (f + 1) * AGG]
            + weight_local[f : f + 1]
            + (weight_back[f : f + 1] + weight_back[f + FACES : f + FACES + 1])
        )
    for entry in range(BLOCK):
        at = slice(entry * 8, entry * 8 + 8)
        value = partial_s[0, at]
        for f in range(FACES):
            value = value + total[f] * partial_s[f + 1, at]
        sums_s[at] = value
    for f in range(FACES):
        sums = pair_sums(
            lambda m, base, f=f: near_s[m, pl.ds((f + 1) * DOFS + base, 16), :],
            lambda n, base, f=f: other_s[f, pl.ds(n * DOFS + base, 16), :],
        )
        negative = -weight[:, f * AGG : (f + 1) * AGG]
        for entry in range(BLOCK):
            at = ((f + 1) * BLOCK + entry) * 8
            sums_s[at : at + 8] = negative * sums[entry]

    coarse_t = sums_s[pl.ds(0, ROW, stride=8), :]
    for s in range(1, 8):
        coarse_t = coarse_t + sums_s[pl.ds(s, ROW, stride=8), :]
    coarse_t = coarse_t.astype(BF16)
    tail = jnp.concatenate([coarse_t[128:], jnp.zeros((256 - ROW, AGG), BF16)], axis=0)
    first = lanes_dot(place_s[...], coarse_t[:128]).reshape(wide_size, CAP, 128)
    second = lanes_dot(place_s[...], tail).reshape(wide_size, CAP, 128)
    send_s[...] = jnp.concatenate([first, second], axis=1).astype(BF16)

    own = pltpu.make_async_copy(send_s.at[w], recv_s.at[w], row_recv)
    own.start()

    def row_copy(k):
        peer = lax.rem(w + k, wide_size)
        return pltpu.make_async_remote_copy(
            src_ref=send_s.at[peer],
            dst_ref=recv_s.at[w],
            send_sem=row_send,
            recv_sem=row_recv,
            device_id=(g, peer),
            device_id_type=MESH,
        )

    def send_rows(k, carry):
        row_copy(k).start()
        return carry

    lax.fori_loop(1, wide_size, send_rows, 0)
    for copy in ghost_copies:
        copy.wait_send()
    pltpu.make_async_copy(recv_s, recv_s, row_recv).wait()

    rows = recv_s[...].astype(F32)
    out_ref[:128, :] = rows[:, :CAP].reshape(wide_size * CAP, 128).T
    out_ref[128:, :] = rows[:, CAP:].reshape(wide_size * CAP, 128).T[: ROW - 128]
    sent = send_s.at[pl.ds(0, wide_size - 1)]
    pltpu.make_async_copy(sent, sent, row_send).wait()


def solution(mesh):
    grp_size, wide_size = mesh.shape["grp"], mesh.shape["wide"]

    def shards(null_space, node_damage, face_target, face_damage, ghost_lists, agg_owner, stiffness):
        coarse = pl.pallas_call(
            functools.partial(kernel, grp_size, wide_size),
            out_shape=jax.ShapeDtypeStruct((ROW, wide_size * CAP), F32),
            in_specs=[pl.BlockSpec(memory_space=pltpu.HBM)] * 7,
            out_specs=pl.BlockSpec(memory_space=pltpu.VMEM),
            scratch_shapes=[
                pltpu.VMEM((AGG, WIDTH), BF16),
                pltpu.VMEM((64, AGG), jnp.int32),
                pltpu.VMEM((FACES, 1, AGG), jnp.int32),
                pltpu.VMEM((FACES, 1, AGG), jnp.int32),
                pltpu.VMEM((4, GHOST), jnp.int32),
                pltpu.VMEM((1, 1, AGG), jnp.int32),
                pltpu.VMEM((DOFS, (1 + FACES) * DOFS), BF16),
                pltpu.VMEM((4, GHOST, MESSAGE), BF16),
                pltpu.VMEM((4, GHOST, MESSAGE), BF16),
                pltpu.VMEM((WIDTH, AGG), BF16),
                pltpu.VMEM(((1 + FACES) * DOFS, DOFS), BF16),
                pltpu.VMEM((MODES, (1 + FACES) * DOFS, AGG), BF16),
                pltpu.VMEM((FACES, WIDTH, AGG), BF16),
                pltpu.VMEM((1 + FACES, BLOCK * 8, AGG), F32),
                pltpu.VMEM((ROW * 8, AGG), F32),
                pltpu.VMEM((wide_size * CAP, AGG), BF16),
                pltpu.VMEM((wide_size, 16, 128), BF16),
                pltpu.VMEM((wide_size, 16, 128), BF16),
                pltpu.SemaphoreType.DMA((7,)),
                pltpu.SemaphoreType.DMA((4,)),
                pltpu.SemaphoreType.DMA((4,)),
                pltpu.SemaphoreType.DMA,
                pltpu.SemaphoreType.DMA,
            ],
            compiler_params=pltpu.CompilerParams(
                collective_id=0, has_side_effects=True, vmem_limit_bytes=32 * 1024 * 1024
            ),
            cost_estimate=pl.CostEstimate(flops=400_000_000, bytes_accessed=1_000_000, transcendentals=0),
        )(
            null_space[0],
            jnp.transpose(node_damage[0]),
            jnp.transpose(face_target, (2, 0, 1)),
            jnp.transpose(face_damage, (2, 0, 1)),
            ghost_lists[0, 0],
            jnp.transpose(agg_owner, (0, 2, 1)),
            stiffness,
        )
        return coarse[None]

    placed = (
        P("grp", "wide", None),
        P("grp", "wide", None),
        P("grp", "wide", None),
        P("grp", "wide", None),
        P("grp", "wide", None, None),
        P("grp", "wide", None),
        P(),
    )
    return jax.shard_map(
        shards, mesh=mesh, in_specs=placed, out_specs=P("grp", "wide", None), check_vma=False
    )
```

```python
import functools

import jax
import jax.numpy as jnp
from jax import lax
from jax.experimental import pallas as pl
from jax.experimental.pallas import tpu as pltpu
from jax.sharding import PartitionSpec as P

AGG = 128
MODES = 6
DOFS = 192
FACES = 3
LEVELS = 8
GHOST = 16
CAP = 8
WIDTH = MODES * DOFS
BLOCK = MODES * MODES
ROW = (1 + FACES) * BLOCK
MESSAGE = WIDTH + 128
MESH = pl.DeviceIdType.MESH
F32 = jnp.float32
BF16 = jnp.bfloat16


def lanes_dot(left, right):
    return lax.dot_general(left, right, (((1,), (1,)), ((), ())), preferred_element_type=F32)


def plain_dot(left, right):
    return jnp.dot(left, right, preferred_element_type=F32)


def ones_where(condition):
    return jnp.where(condition, 1.0, 0.0).astype(BF16)


def iota(shape, dim):
    return lax.broadcasted_iota(jnp.int32, shape, dim)


def pair_sums(load_left, load_right):
    def step(i, sums):
        base = pl.multiple_of(i * 16, 16)
        left = [load_left(m, base).astype(F32) for m in range(MODES)]
        right = [load_right(n, base).astype(F32) for n in range(MODES)]
        new = []
        for m in range(MODES):
            for n in range(MODES):
                product = left[m] * right[n]
                new.append(sums[m * MODES + n] + (product[:8] + product[8:]))
        return tuple(new)

    zero = jnp.zeros((8, AGG), F32)
    return lax.fori_loop(0, DOFS // 16, step, (zero,) * BLOCK)


def kernel(
    grp_size, wide_size,
    null_hbm, damage_hbm, target_hbm, face_hbm, list_hbm, owner_hbm, stiff_hbm,
    out_ref,
    null_v, damage_v, target_v, face_v, list_v, owner_v, stiff_v,
    message_out, message_in, modes_t, stiff_t, near_s, other_s, partial_s, sums_s, place_s, send_s, recv_s,
    in_sem, ghost_send, ghost_recv, row_send, row_recv, everyone,
):
    g = lax.axis_index("grp")
    w = lax.axis_index("wide")

    barrier = pltpu.get_barrier_semaphore()
    neighbours = [(g - 1, w), (g + 1, w), (g, w - 1), (g, w + 1)]
    valid = [g > 0, g < grp_size - 1, w > 0, w < wide_size - 1]
    hubs = (wide_size // 2, wide_size - 1)
    is_hub = (w == hubs[0]) | (w == hubs[1])

    def greet(peer, condition):
        @pl.when(condition)
        def _():
            pl.semaphore_signal(barrier, inc=1, device_id=peer, device_id_type=MESH)

    for peer, condition in zip(neighbours, valid):
        greet(peer, condition)
    for hub in hubs:
        greet((g, hub), w != hub)

    loads = [
        pltpu.make_async_copy(source, target, in_sem.at[k])
        for k, (source, target) in enumerate(
            [
                (list_hbm, list_v), (damage_hbm, damage_v), (null_hbm, null_v), (target_hbm, target_v),
                (face_hbm, face_v), (owner_hbm, owner_v), (stiff_hbm, stiff_v),
            ]
        )
    ]
    for load in loads:
        load.start()

    loads[0].wait()
    listed = list_v[...].astype(F32)
    spread = jnp.concatenate([jnp.broadcast_to(listed[r : r + 1], (GHOST, GHOST)) for r in range(4)], axis=0)
    on_diagonal = (iota((4 * GHOST, GHOST), 0) & (GHOST - 1)) == iota((4 * GHOST, GHOST), 1)
    list_column = jnp.sum(jnp.where(on_diagonal, spread, 0.0), axis=1, keepdims=True).astype(jnp.int32)
    select = ones_where(list_column == iota((4 * GHOST, AGG), 1))

    loads[1].wait()
    levels = ((LEVELS - damage_v[...]).astype(F32) * (1.0 / LEVELS)).T.astype(BF16)
    node_of = ((iota((1, WIDTH), 1) * 43691) >> 17) & 63
    widen = ones_where(iota((64, WIDTH), 0) == node_of)
    scales = plain_dot(levels, widen)
    loads[2].wait()
    modes = (null_v[...].astype(F32) * scales).astype(BF16)
    picked = plain_dot(select, modes).astype(BF16)

    loads[3].wait()
    loads[4].wait()
    targets = jnp.concatenate([target_v[f] for f in range(FACES)], axis=1)
    levels_f = jnp.concatenate([face_v[f] for f in range(FACES)], axis=1)
    level = (LEVELS - levels_f).astype(F32) * (1.0 / LEVELS)
    weight = level * level
    chosen = ones_where(iota((AGG + 4 * GHOST, FACES * AGG), 0) == targets)
    row = iota((AGG, FACES * AGG), 0)
    face_of = iota((AGG, FACES * AGG), 1) >> 7
    weight_rows = jnp.where((row == face_of) | (row == face_of + FACES), weight, 0.0).astype(BF16)
    weight_local = lanes_dot(weight_rows[:16], chosen[:AGG])
    weight_ghost = lanes_dot(chosen[AGG:], weight_rows)
    high = weight_ghost.astype(BF16).astype(F32)
    split = jnp.where(iota((4 * GHOST, 128), 1) < FACES, high, weight_ghost - high).astype(BF16)
    for r in range(4):
        message_out[r, :, :WIDTH] = picked[r * GHOST : (r + 1) * GHOST]
        message_out[r, :, WIDTH:] = split[r * GHOST : (r + 1) * GHOST]

    for r in range(4):
        @pl.when(jnp.logical_not(valid[r]))
        def _(r=r):
            message_in[r] = jnp.zeros((GHOST, MESSAGE), BF16)

    near_count = sum(condition.astype(jnp.int32) for condition in valid)
    pl.semaphore_wait(barrier, near_count + is_hub.astype(jnp.int32) * (wide_size - 1))
    ghost_copies = [
        pltpu.make_async_remote_copy(
            src_ref=message_out.at[r],
            dst_ref=message_in.at[r ^ 1],
            send_sem=ghost_send.at[r],
            recv_sem=ghost_recv.at[r ^ 1],
            device_id=neighbours[r],
            device_id_type=MESH,
        )
        for r in range(4)
    ]
    for r in range(4):
        pl.when(valid[r])(ghost_copies[r].start)

    @pl.when(is_hub)
    def _():
        first_told = jnp.where(w == hubs[0], wide_size // 4, wide_size // 4 * 3)

        def tell(k, carry):
            peer = lax.rem(first_told + k, wide_size)

            @pl.when(peer != w)
            def _():
                pl.semaphore_signal(everyone, inc=1, device_id=(g, peer), device_id_type=MESH)

            return carry

        lax.fori_loop(0, wide_size // 2, tell, 0)

    modes_t[...] = modes.T
    loads[6].wait()
    stiff_t[...] = stiff_v[...].T
    for pair in range(MODES // 2):
        two = jnp.concatenate(
            [modes_t[(2 * pair + h) * DOFS : (2 * pair + h + 1) * DOFS] for h in range(2)], axis=1
        )
        product = plain_dot(stiff_t[...], two).astype(BF16)
        near_s[2 * pair] = product[:, :AGG]
        near_s[2 * pair + 1] = product[:, AGG:]

    loads[5].wait()
    owner = owner_v[0]
    owned = iota((wide_size, AGG), 0) == owner
    before = ones_where(iota((AGG, AGG), 0) < iota((AGG, AGG), 1))
    earlier = plain_dot(ones_where(owned), before)
    rank = jnp.sum(jnp.where(owned, earlier, 0.0), axis=0, keepdims=True).astype(jnp.int32)
    place_s[...] = ones_where(iota((wide_size * CAP, AGG), 0) == owner * CAP + rank)

    def load_modes(m, base):
        return modes_t[pl.ds(m * DOFS + base, 16), :]

    for k in range(1 + FACES):
        sums = pair_sums(lambda m, base, k=k: near_s[m, pl.ds(k * DOFS + base, 16), :], load_modes)
        for entry in range(BLOCK):
            partial_s[k, entry * 8 : entry * 8 + 8] = sums[entry]

    for r in range(4):
        pl.when(valid[r])(ghost_copies[r ^ 1].wait_recv)
    arrived = jnp.concatenate([message_in[r] for r in range(4)], axis=0)
    arrived_t = arrived.T
    ghosts_t = arrived_t[:WIDTH]
    weight_back = plain_dot(arrived_t[WIDTH : WIDTH + 16], select)
    for f in range(FACES):
        at = slice(f * AGG, (f + 1) * AGG)
        other = plain_dot(modes_t[...], chosen[:AGG, at]) + plain_dot(ghosts_t, chosen[AGG:, at])
        other_s[f] = other.astype(BF16)

    total = []
    for f in range(FACES):
        total.append(
            weight[:, f * AGG : (f + 1) * AGG]
            + weight_local[f : f + 1]
            + (weight_back[f : f + 1] + weight_back[f + FACES : f + FACES + 1])
        )
    for entry in range(BLOCK):
        at = slice(entry * 8, entry * 8 + 8)
        value = partial_s[0, at]
        for f in range(FACES):
            value = value + total[f] * partial_s[f + 1, at]
        sums_s[at] = value
    for f in range(FACES):
        sums = pair_sums(
            lambda m, base, f=f: near_s[m, pl.ds((f + 1) * DOFS + base, 16), :],
            lambda n, base, f=f: other_s[f, pl.ds(n * DOFS + base, 16), :],
        )
        negative = -weight[:, f * AGG : (f + 1) * AGG]
        for entry in range(BLOCK):
            at = ((f + 1) * BLOCK + entry) * 8
            sums_s[at : at + 8] = negative * sums[entry]

    coarse_t = sums_s[pl.ds(0, ROW, stride=8), :]
    for s in range(1, 8):
        coarse_t = coarse_t + sums_s[pl.ds(s, ROW, stride=8), :]
    coarse_t = coarse_t.astype(BF16)
    tail = jnp.concatenate([coarse_t[128:], jnp.zeros((256 - ROW, AGG), BF16)], axis=0)
    first = lanes_dot(place_s[...], coarse_t[:128]).reshape(wide_size, CAP, 128)
    second = lanes_dot(place_s[...], tail).reshape(wide_size, CAP, 128)
    send_s[...] = jnp.concatenate([first, second], axis=1).astype(BF16)

    pl.when(jnp.logical_not(is_hub))(lambda: pl.semaphore_wait(everyone, 1))
    own = pltpu.make_async_copy(send_s.at[w], recv_s.at[w], row_recv)
    own.start()

    def row_copy(k):
        peer = lax.rem(w + k, wide_size)
        return pltpu.make_async_remote_copy(
            src_ref=send_s.at[peer],
            dst_ref=recv_s.at[w],
            send_sem=row_send,
            recv_sem=row_recv,
            device_id=(g, peer),
            device_id_type=MESH,
        )

    def send_rows(k, carry):
        row_copy(k).start()
        return carry

    lax.fori_loop(1, wide_size, send_rows, 0)
    for r in range(4):
        pl.when(valid[r])(ghost_copies[r].wait_send)
    pltpu.make_async_copy(recv_s, recv_s, row_recv).wait()

    rows = recv_s[...].astype(F32)
    out_ref[:128, :] = rows[:, :CAP].reshape(wide_size * CAP, 128).T
    out_ref[128:, :] = rows[:, CAP:].reshape(wide_size * CAP, 128).T[: ROW - 128]
    sent = send_s.at[pl.ds(0, wide_size - 1)]
    pltpu.make_async_copy(sent, sent, row_send).wait()


def solution(mesh):
    grp_size, wide_size = mesh.shape["grp"], mesh.shape["wide"]

    def shards(null_space, node_damage, face_target, face_damage, ghost_lists, agg_owner, stiffness):
        coarse = pl.pallas_call(
            functools.partial(kernel, grp_size, wide_size),
            out_shape=jax.ShapeDtypeStruct((ROW, wide_size * CAP), F32),
            in_specs=[pl.BlockSpec(memory_space=pltpu.HBM)] * 7,
            out_specs=pl.BlockSpec(memory_space=pltpu.VMEM),
            scratch_shapes=[
                pltpu.VMEM((AGG, WIDTH), BF16),
                pltpu.VMEM((64, AGG), jnp.int32),
                pltpu.VMEM((FACES, 1, AGG), jnp.int32),
                pltpu.VMEM((FACES, 1, AGG), jnp.int32),
                pltpu.VMEM((4, GHOST), jnp.int32),
                pltpu.VMEM((1, 1, AGG), jnp.int32),
                pltpu.VMEM((DOFS, (1 + FACES) * DOFS), BF16),
                pltpu.VMEM((4, GHOST, MESSAGE), BF16),
                pltpu.VMEM((4, GHOST, MESSAGE), BF16),
                pltpu.VMEM((WIDTH, AGG), BF16),
                pltpu.VMEM(((1 + FACES) * DOFS, DOFS), BF16),
                pltpu.VMEM((MODES, (1 + FACES) * DOFS, AGG), BF16),
                pltpu.VMEM((FACES, WIDTH, AGG), BF16),
                pltpu.VMEM((1 + FACES, BLOCK * 8, AGG), F32),
                pltpu.VMEM((ROW * 8, AGG), F32),
                pltpu.VMEM((wide_size * CAP, AGG), BF16),
                pltpu.VMEM((wide_size, 16, 128), BF16),
                pltpu.VMEM((wide_size, 16, 128), BF16),
                pltpu.SemaphoreType.DMA((7,)),
                pltpu.SemaphoreType.DMA((4,)),
                pltpu.SemaphoreType.DMA((4,)),
                pltpu.SemaphoreType.DMA,
                pltpu.SemaphoreType.DMA,
                pltpu.SemaphoreType.REGULAR,
            ],
            compiler_params=pltpu.CompilerParams(
                collective_id=0, has_side_effects=True, vmem_limit_bytes=56 * 1024 * 1024
            ),
            cost_estimate=pl.CostEstimate(flops=400_000_000, bytes_accessed=1_000_000, transcendentals=0),
        )(
            null_space[0],
            jnp.transpose(node_damage[0]),
            jnp.transpose(face_target, (2, 0, 1)),
            jnp.transpose(face_damage, (2, 0, 1)),
            ghost_lists[0, 0],
            jnp.transpose(agg_owner, (0, 2, 1)),
            stiffness,
        )
        return coarse[None]

    placed = (
        P("grp", "wide", None),
        P("grp", "wide", None),
        P("grp", "wide", None),
        P("grp", "wide", None),
        P("grp", "wide", None, None),
        P("grp", "wide", None),
        P(),
    )
    return jax.shard_map(
        shards, mesh=mesh, in_specs=placed, out_specs=P("grp", "wide", None), check_vma=False
    )
```

```python
import functools

import jax
import jax.numpy as jnp
from jax import lax
from jax.experimental import pallas as pl
from jax.experimental.pallas import tpu as pltpu
from jax.sharding import PartitionSpec as P

AGG = 128
MODES = 6
DOFS = 192
FACES = 3
LEVELS = 8
GHOST = 16
CAP = 8
WIDTH = MODES * DOFS
BLOCK = MODES * MODES
ROW = (1 + FACES) * BLOCK
MESSAGE = WIDTH + 128
MESH = pl.DeviceIdType.MESH
F32 = jnp.float32
BF16 = jnp.bfloat16


def lanes_dot(left, right):
    return lax.dot_general(left, right, (((1,), (1,)), ((), ())), preferred_element_type=F32)


def plain_dot(left, right):
    return jnp.dot(left, right, preferred_element_type=F32)


def ones_where(condition):
    return jnp.where(condition, 1.0, 0.0).astype(BF16)


def iota(shape, dim):
    return lax.broadcasted_iota(jnp.int32, shape, dim)


def pair_sums(load_left, load_right):
    def step(i, sums):
        base = pl.multiple_of(i * 16, 16)
        left = [load_left(m, base).astype(F32) for m in range(MODES)]
        right = [load_right(n, base).astype(F32) for n in range(MODES)]
        new = []
        for m in range(MODES):
            for n in range(MODES):
                product = left[m] * right[n]
                new.append(sums[m * MODES + n] + (product[:8] + product[8:]))
        return tuple(new)

    zero = jnp.zeros((8, AGG), F32)
    return lax.fori_loop(0, DOFS // 16, step, (zero,) * BLOCK)


def row_sums(parts):
    sub = iota((8, AGG), 0)

    def halves(low, high, bit):
        low = low + pltpu.roll(low, 8 - bit, 0)
        high = high + pltpu.roll(high, bit, 0)
        return jnp.where((sub & bit) == 0, low, high)

    for bit in (4, 2, 1):
        count = len(parts) // 2
        parts = [halves(parts[i], parts[i + count], bit) for i in range(count)]
    return parts[0]


def kernel(
    grp_size, wide_size,
    null_hbm, damage_hbm, target_hbm, face_hbm, list_hbm, owner_hbm, stiff_hbm,
    out_ref,
    null_v, damage_v, target_v, face_v, list_v, owner_v, stiff_v,
    message_out, message_in, modes_t, stiff_t, near_s, other_s, diag_s, partial_s, place_s, send_s, recv_s,
    in_sem, ghost_send, ghost_recv, row_send, row_recv, everyone,
):
    g = lax.axis_index("grp")
    w = lax.axis_index("wide")

    barrier = pltpu.get_barrier_semaphore()
    neighbours = [(g - 1, w), (g + 1, w), (g, w - 1), (g, w + 1)]
    valid = [g > 0, g < grp_size - 1, w > 0, w < wide_size - 1]
    hubs = (wide_size // 2, wide_size - 1)
    is_hub = (w == hubs[0]) | (w == hubs[1])

    def greet(peer, condition):
        @pl.when(condition)
        def _():
            pl.semaphore_signal(barrier, inc=1, device_id=peer, device_id_type=MESH)

    for peer, condition in zip(neighbours, valid):
        greet(peer, condition)
    for hub in hubs:
        greet((g, hub), w != hub)

    loads = [
        pltpu.make_async_copy(source, target, in_sem.at[k])
        for k, (source, target) in enumerate(
            [
                (list_hbm, list_v), (damage_hbm, damage_v), (null_hbm, null_v), (target_hbm, target_v),
                (face_hbm, face_v), (owner_hbm, owner_v), (stiff_hbm, stiff_v),
            ]
        )
    ]
    for load in loads:
        load.start()

    loads[0].wait()
    listed = list_v[...].astype(F32)
    spread = jnp.concatenate([jnp.broadcast_to(listed[r : r + 1], (GHOST, GHOST)) for r in range(4)], axis=0)
    on_diagonal = (iota((4 * GHOST, GHOST), 0) & (GHOST - 1)) == iota((4 * GHOST, GHOST), 1)
    list_column = jnp.sum(jnp.where(on_diagonal, spread, 0.0), axis=1, keepdims=True).astype(jnp.int32)
    select = ones_where(list_column == iota((4 * GHOST, AGG), 1))

    loads[1].wait()
    levels = ((LEVELS - damage_v[...]).astype(F32) * (1.0 / LEVELS)).T.astype(BF16)
    node_of = ((iota((1, WIDTH), 1) * 43691) >> 17) & 63
    widen = ones_where(iota((64, WIDTH), 0) == node_of)
    scales = plain_dot(levels, widen)
    loads[2].wait()
    modes = (null_v[...].astype(F32) * scales).astype(BF16)
    picked = plain_dot(select, modes).astype(BF16)

    loads[3].wait()
    loads[4].wait()
    targets = jnp.concatenate([target_v[f] for f in range(FACES)], axis=1)
    levels_f = jnp.concatenate([face_v[f] for f in range(FACES)], axis=1)
    level = (LEVELS - levels_f).astype(F32) * (1.0 / LEVELS)
    weight = level * level
    chosen = ones_where(iota((AGG + 4 * GHOST, FACES * AGG), 0) == targets)
    row = iota((AGG, FACES * AGG), 0)
    face_of = iota((AGG, FACES * AGG), 1) >> 7
    weight_rows = jnp.where((row == face_of) | (row == face_of + FACES), weight, 0.0).astype(BF16)
    weight_local = lanes_dot(weight_rows[:16], chosen[:AGG])
    weight_ghost = lanes_dot(chosen[AGG:], weight_rows)
    high = weight_ghost.astype(BF16).astype(F32)
    split = jnp.where(iota((4 * GHOST, 128), 1) < FACES, high, weight_ghost - high).astype(BF16)
    for r in range(4):
        message_out[r, :, :WIDTH] = picked[r * GHOST : (r + 1) * GHOST]
        message_out[r, :, WIDTH:] = split[r * GHOST : (r + 1) * GHOST]

    for r in range(4):
        @pl.when(jnp.logical_not(valid[r]))
        def _(r=r):
            message_in[r] = jnp.zeros((GHOST, MESSAGE), BF16)

    near_count = sum(condition.astype(jnp.int32) for condition in valid)
    pl.semaphore_wait(barrier, near_count + is_hub.astype(jnp.int32) * (wide_size - 1))
    ghost_copies = [
        pltpu.make_async_remote_copy(
            src_ref=message_out.at[r],
            dst_ref=message_in.at[r ^ 1],
            send_sem=ghost_send.at[r],
            recv_sem=ghost_recv.at[r ^ 1],
            device_id=neighbours[r],
            device_id_type=MESH,
        )
        for r in range(4)
    ]
    for r in range(4):
        pl.when(valid[r])(ghost_copies[r].start)

    @pl.when(is_hub)
    def _():
        first_told = jnp.where(w == hubs[0], wide_size // 4, wide_size // 4 * 3)

        def tell(k, carry):
            peer = lax.rem(first_told + k, wide_size)

            @pl.when(peer != w)
            def _():
                pl.semaphore_signal(everyone, inc=1, device_id=(g, peer), device_id_type=MESH)

            return carry

        lax.fori_loop(0, wide_size // 2, tell, 0)

    modes_t[...] = modes.T
    loads[6].wait()
    stiff_t[...] = stiff_v[...].T
    for pair in range(MODES // 2):
        two = jnp.concatenate(
            [modes_t[(2 * pair + h) * DOFS : (2 * pair + h + 1) * DOFS] for h in range(2)], axis=1
        )
        near_s[pair] = plain_dot(stiff_t[...], two).astype(BF16)
    for f in range(FACES):
        other_s[f] = plain_dot(modes_t[...], chosen[:AGG, f * AGG : (f + 1) * AGG]).astype(BF16)

    loads[5].wait()
    owner = owner_v[0]
    owned = iota((wide_size, AGG), 0) == owner
    owned_ones = ones_where(owned)
    before = ones_where(iota((AGG, AGG), 0) < iota((AGG, AGG), 1))
    earlier = plain_dot(owned_ones, before)
    rank = jnp.sum(jnp.where(owned, earlier, 0.0), axis=0, keepdims=True).astype(jnp.int32)
    place_s[...] = ones_where(iota((wide_size * CAP, AGG), 0) == owner * CAP + rank)

    def load_near(k):
        def load(m, base):
            return near_s[m // 2, pl.ds(k * DOFS + base, 16), m % 2 * AGG : (m % 2 + 1) * AGG]

        return load

    def load_modes(m, base):
        return modes_t[pl.ds(m * DOFS + base, 16), :]

    zero = jnp.zeros((8, AGG), F32)
    for k in range(1 + FACES):
        sums = list(pair_sums(load_near(k), load_modes)) + [zero] * 4
        for entry in range(0, BLOCK, 8):
            diag_s[k, entry : entry + 8] = row_sums(sums[entry : entry + 8])
    for f in range(FACES):
        sums = pair_sums(load_near(f + 1), lambda n, base, f=f: other_s[f, pl.ds(n * DOFS + base, 16), :])
        for entry in range(BLOCK):
            partial_s[f, entry * 8 : entry * 8 + 8] = sums[entry]

    for r in range(4):
        pl.when(valid[r])(ghost_copies[r ^ 1].wait_recv)
    arrived = jnp.concatenate([message_in[r] for r in range(4)], axis=0)
    ghosts = jnp.concatenate([arrived[:, n * DOFS : (n + 1) * DOFS] for n in range(MODES)], axis=0)
    weight_back = plain_dot(arrived[:, WIDTH:].T[:16], select)
    parts = [zero] * 4
    scale = []
    for f in range(FACES):
        target = jnp.broadcast_to(targets[:, f * AGG : (f + 1) * AGG], (8, AGG)) - AGG
        wanted = [iota((8, AGG), 0) + 8 * group == target for group in range(4 * GHOST // 8)]
        for pair in range(MODES // 2):
            product = plain_dot(ghosts, near_s[pair, (f + 1) * DOFS : (f + 2) * DOFS])
            for half in range(2):
                for n in range(MODES):
                    taken = zero
                    for group, mask in enumerate(wanted):
                        at = n * 4 * GHOST + group * 8
                        taken = jnp.where(mask, product[at : at + 8, half * AGG : (half + 1) * AGG], taken)
                    entry = (2 * pair + half) * MODES + n
                    parts.append(partial_s[f, entry * 8 : entry * 8 + 8] + taken)

    total = []
    for f in range(FACES):
        total.append(
            weight[:, f * AGG : (f + 1) * AGG]
            + weight_local[f : f + 1]
            + (weight_back[f : f + 1] + weight_back[f + FACES : f + FACES + 1])
        )
    diag = diag_s[0]
    for f in range(FACES):
        diag = diag + total[f] * diag_s[f + 1]
    faces = jnp.concatenate([row_sums(parts[e : e + 8]) for e in range(0, FACES * BLOCK + 4, 8)], axis=0)
    factor = jnp.concatenate(
        [jnp.zeros((4, AGG), F32)]
        + [jnp.broadcast_to(-weight[:, f * AGG : (f + 1) * AGG], (BLOCK, AGG)) for f in range(FACES)],
        axis=0,
    )
    faces = faces * factor
    coarse_t = jnp.concatenate([diag[:32], diag[32:] + faces[:8], faces[8:]], axis=0)

    first = lanes_dot(place_s[...], coarse_t[:128].astype(BF16)).astype(BF16)
    last = jnp.concatenate([jnp.where(rank == s, coarse_t[128:], 0.0) for s in range(CAP)], axis=0).astype(BF16)
    last = lanes_dot(owned_ones, last)
    send_s[:, :4] = first.reshape(wide_size, 4, 2, 128)
    send_s[:, 4] = jnp.concatenate([last[:, None], jnp.zeros((wide_size, 1, 128), F32)], axis=1).astype(BF16)

    pl.when(jnp.logical_not(is_hub))(lambda: pl.semaphore_wait(everyone, 1))

    def send_rows(i, carry):
        k = wide_size - 2 - i
        step = k // 2 + 1
        peer = lax.rem(w + step + lax.rem(k, 2) * (wide_size - 2 * step), wide_size)
        pltpu.make_async_remote_copy(
            src_ref=send_s.at[peer],
            dst_ref=recv_s.at[w],
            send_sem=row_send,
            recv_sem=row_recv,
            device_id=(g, peer),
            device_id_type=MESH,
        ).start()
        return carry

    lax.fori_loop(0, wide_size - 1, send_rows, 0)
    pltpu.make_async_copy(send_s.at[w], recv_s.at[w], row_recv).start()
    for r in range(4):
        pl.when(valid[r])(ghost_copies[r].wait_send)
    column = iota((wide_size, wide_size * CAP), 1)
    sender = ones_where(column // CAP == iota((wide_size, wide_size * CAP), 0))
    pltpu.make_async_copy(recv_s, recv_s, row_recv).wait()

    out_ref[:128, :] = recv_s[:, :4].reshape(wide_size * CAP, 128).T.astype(F32)
    last = plain_dot(recv_s[:, 4].astype(F32)[:, 0].T.astype(BF16), sender)
    slot = lax.rem(iota((16, wide_size * CAP), 1), CAP)
    tail = jnp.zeros((16, wide_size * CAP), F32)
    for s in range(CAP):
        tail = jnp.where(slot == s, last[s * 16 : (s + 1) * 16], tail)
    out_ref[128:, :] = tail
    sent = send_s.at[pl.ds(0, wide_size - 1)]
    pltpu.make_async_copy(sent, sent, row_send).wait()


def solution(mesh):
    grp_size, wide_size = mesh.shape["grp"], mesh.shape["wide"]

    def shards(null_space, node_damage, face_target, face_damage, ghost_lists, agg_owner, stiffness):
        coarse = pl.pallas_call(
            functools.partial(kernel, grp_size, wide_size),
            out_shape=pltpu.VMEM((ROW, wide_size * CAP), F32),
            in_specs=[pl.BlockSpec(memory_space=pltpu.HBM)] * 7,
            out_specs=pl.BlockSpec(memory_space=pltpu.VMEM),
            scratch_shapes=[
                pltpu.VMEM((AGG, WIDTH), BF16),
                pltpu.VMEM((64, AGG), jnp.int32),
                pltpu.VMEM((FACES, 1, AGG), jnp.int32),
                pltpu.VMEM((FACES, 1, AGG), jnp.int32),
                pltpu.VMEM((4, GHOST), jnp.int32),
                pltpu.VMEM((1, 1, AGG), jnp.int32),
                pltpu.VMEM((DOFS, (1 + FACES) * DOFS), BF16),
                pltpu.VMEM((4, GHOST, MESSAGE), BF16),
                pltpu.VMEM((4, GHOST, MESSAGE), BF16),
                pltpu.VMEM((WIDTH, AGG), BF16),
                pltpu.VMEM(((1 + FACES) * DOFS, DOFS), BF16),
                pltpu.VMEM((MODES // 2, (1 + FACES) * DOFS, 2 * AGG), BF16),
                pltpu.VMEM((FACES, WIDTH, AGG), BF16),
                pltpu.VMEM((1 + FACES, BLOCK + 4, AGG), F32),
                pltpu.VMEM((FACES, BLOCK * 8, AGG), F32),
                pltpu.VMEM((wide_size * CAP, AGG), BF16),
                pltpu.VMEM((wide_size, 5, 2, 128), BF16),
                pltpu.VMEM((wide_size, 5, 2, 128), BF16),
                pltpu.SemaphoreType.DMA((7,)),
                pltpu.SemaphoreType.DMA((4,)),
                pltpu.SemaphoreType.DMA((4,)),
                pltpu.SemaphoreType.DMA,
                pltpu.SemaphoreType.DMA,
                pltpu.SemaphoreType.REGULAR,
            ],
            compiler_params=pltpu.CompilerParams(
                collective_id=0, has_side_effects=True, vmem_limit_bytes=56 * 1024 * 1024
            ),
            cost_estimate=pl.CostEstimate(flops=400_000_000, bytes_accessed=1_000_000, transcendentals=0),
        )(
            null_space[0],
            jnp.transpose(node_damage[0]),
            jnp.transpose(face_target, (2, 0, 1)),
            jnp.transpose(face_damage, (2, 0, 1)),
            ghost_lists[0, 0],
            jnp.transpose(agg_owner, (0, 2, 1)),
            stiffness,
        )
        return coarse[None]

    placed = (
        P("grp", "wide", None),
        P("grp", "wide", None),
        P("grp", "wide", None),
        P("grp", "wide", None),
        P("grp", "wide", None, None),
        P("grp", "wide", None),
        P(),
    )
    return jax.shard_map(
        shards, mesh=mesh, in_specs=placed, out_specs=P("grp", "wide", None), check_vma=False
    )
```

```python
import functools

import jax
import jax.numpy as jnp
from jax import lax
from jax.experimental import pallas as pl
from jax.experimental.pallas import tpu as pltpu
from jax.sharding import PartitionSpec as P

AGG = 128
MODES = 6
DOFS = 192
FACES = 3
LEVELS = 8
GHOST = 16
CAP = 8
WIDTH = MODES * DOFS
BLOCK = MODES * MODES
ROW = (1 + FACES) * BLOCK
MESSAGE = WIDTH + 128
MESH = pl.DeviceIdType.MESH
F32 = jnp.float32
BF16 = jnp.bfloat16


def lanes_dot(left, right):
    return lax.dot_general(left, right, (((1,), (1,)), ((), ())), preferred_element_type=F32)


def plain_dot(left, right):
    return jnp.dot(left, right, preferred_element_type=F32)


def ones_where(condition):
    return jnp.where(condition, 1.0, 0.0).astype(BF16)


def iota(shape, dim):
    return lax.broadcasted_iota(jnp.int32, shape, dim)


def pair_sums(load_left, load_right):
    def step(i, sums):
        base = pl.multiple_of(i * 16, 16)
        left = [load_left(m, base).astype(F32) for m in range(MODES)]
        right = [load_right(n, base).astype(F32) for n in range(MODES)]
        new = []
        for m in range(MODES):
            for n in range(MODES):
                product = left[m] * right[n]
                new.append(sums[m * MODES + n] + (product[:8] + product[8:]))
        return tuple(new)

    zero = jnp.zeros((8, AGG), F32)
    return lax.fori_loop(0, DOFS // 16, step, (zero,) * BLOCK, unroll=True)


def row_sums(parts):
    sub = iota((8, AGG), 0)

    def halves(low, high, bit):
        low = low + pltpu.roll(low, 8 - bit, 0)
        high = high + pltpu.roll(high, bit, 0)
        return jnp.where((sub & bit) == 0, low, high)

    for bit in (4, 2, 1):
        count = len(parts) // 2
        parts = [halves(parts[i], parts[i + count], bit) for i in range(count)]
    return parts[0]


def kernel(
    grp_size, wide_size,
    null_hbm, damage_hbm, target_hbm, face_hbm, list_hbm, owner_hbm, stiff_hbm,
    out_ref,
    null_v, damage_v, target_v, face_v, list_v, owner_v, stiff_v,
    message_out, message_in, modes_t, stiff_t, near_s, other_s, diag_s, partial_s, place_s, send_s, recv_s,
    in_sem, ghost_send, ghost_recv, row_send, row_recv, everyone,
):
    g = lax.axis_index("grp")
    w = lax.axis_index("wide")

    barrier = pltpu.get_barrier_semaphore()
    neighbours = [(g - 1, w), (g + 1, w), (g, w - 1), (g, w + 1)]
    valid = [g > 0, g < grp_size - 1, w > 0, w < wide_size - 1]
    hub = wide_size * 23 // 32
    is_hub = w == hub

    def greet(peer, condition):
        @pl.when(condition)
        def _():
            pl.semaphore_signal(barrier, inc=1, device_id=peer, device_id_type=MESH)

    for peer, condition in zip(neighbours, valid):
        greet(peer, condition)
    greet((g, hub), w != hub)

    loads = [
        pltpu.make_async_copy(source, target, in_sem.at[k])
        for k, (source, target) in enumerate(
            [
                (list_hbm, list_v), (damage_hbm, damage_v), (null_hbm, null_v), (target_hbm, target_v),
                (face_hbm, face_v), (owner_hbm, owner_v), (stiff_hbm, stiff_v),
            ]
        )
    ]
    for load in loads:
        load.start()

    loads[0].wait()
    listed = list_v[...].astype(F32)
    spread = jnp.concatenate([jnp.broadcast_to(listed[r : r + 1], (GHOST, GHOST)) for r in range(4)], axis=0)
    on_diagonal = (iota((4 * GHOST, GHOST), 0) & (GHOST - 1)) == iota((4 * GHOST, GHOST), 1)
    list_column = jnp.sum(jnp.where(on_diagonal, spread, 0.0), axis=1, keepdims=True).astype(jnp.int32)
    select = ones_where(list_column == iota((4 * GHOST, AGG), 1))

    loads[1].wait()
    levels = ((LEVELS - damage_v[...]).astype(F32) * (1.0 / LEVELS)).T.astype(BF16)
    node_of = ((iota((1, WIDTH), 1) * 43691) >> 17) & 63
    widen = ones_where(iota((64, WIDTH), 0) == node_of)
    scales = plain_dot(levels, widen)
    loads[2].wait()
    modes = (null_v[...].astype(F32) * scales).astype(BF16)
    picked = plain_dot(select, modes).astype(BF16)

    loads[3].wait()
    loads[4].wait()
    targets = jnp.concatenate([target_v[f] for f in range(FACES)], axis=1)
    levels_f = jnp.concatenate([face_v[f] for f in range(FACES)], axis=1)
    level = (LEVELS - levels_f).astype(F32) * (1.0 / LEVELS)
    weight = level * level
    chosen = ones_where(iota((AGG + 4 * GHOST, FACES * AGG), 0) == targets)
    row = iota((AGG, FACES * AGG), 0)
    face_of = iota((AGG, FACES * AGG), 1) >> 7
    weight_rows = jnp.where((row == face_of) | (row == face_of + FACES), weight, 0.0).astype(BF16)
    weight_local = lanes_dot(weight_rows[:16], chosen[:AGG])
    weight_ghost = lanes_dot(chosen[AGG:], weight_rows)
    high = weight_ghost.astype(BF16).astype(F32)
    split = jnp.where(iota((4 * GHOST, 128), 1) < FACES, high, weight_ghost - high).astype(BF16)
    for r in range(4):
        message_out[r, :, :WIDTH] = picked[r * GHOST : (r + 1) * GHOST]
        message_out[r, :, WIDTH:] = split[r * GHOST : (r + 1) * GHOST]

    for r in range(4):
        @pl.when(jnp.logical_not(valid[r]))
        def _(r=r):
            message_in[r] = jnp.zeros((GHOST, MESSAGE), BF16)

    near_count = sum(condition.astype(jnp.int32) for condition in valid)
    pl.semaphore_wait(barrier, near_count + is_hub.astype(jnp.int32) * (wide_size - 1))
    ghost_copies = [
        pltpu.make_async_remote_copy(
            src_ref=message_out.at[r],
            dst_ref=message_in.at[r ^ 1],
            send_sem=ghost_send.at[r],
            recv_sem=ghost_recv.at[r ^ 1],
            device_id=neighbours[r],
            device_id_type=MESH,
        )
        for r in range(4)
    ]
    for r in range(4):
        pl.when(valid[r])(ghost_copies[r].start)

    def partner(i):
        k = wide_size - 2 - i
        step = k // 2 + 1
        return lax.rem(w + step + lax.rem(k, 2) * (wide_size - 2 * step), wide_size)

    @pl.when(is_hub)
    def _():
        def tell(i, carry):
            pl.semaphore_signal(everyone, inc=1, device_id=(g, partner(i)), device_id_type=MESH)
            return carry

        lax.fori_loop(0, wide_size - 1, tell, 0)

    modes_t[...] = modes.T
    loads[6].wait()
    stiff_t[...] = stiff_v[...].T
    for pair in range(MODES // 2):
        two = jnp.concatenate(
            [modes_t[(2 * pair + h) * DOFS : (2 * pair + h + 1) * DOFS] for h in range(2)], axis=1
        )
        near_s[pair] = plain_dot(stiff_t[...], two).astype(BF16)
    for f in range(FACES):
        other_s[f] = plain_dot(modes_t[...], chosen[:AGG, f * AGG : (f + 1) * AGG]).astype(BF16)

    loads[5].wait()
    owner = owner_v[0]
    owned = iota((wide_size, AGG), 0) == owner
    owned_ones = ones_where(owned)
    before = ones_where(iota((AGG, AGG), 0) < iota((AGG, AGG), 1))
    earlier = plain_dot(owned_ones, before)
    rank = jnp.sum(jnp.where(owned, earlier, 0.0), axis=0, keepdims=True).astype(jnp.int32)
    place_s[...] = ones_where(iota((wide_size * CAP, AGG), 0) == owner * CAP + rank)

    def load_near(k):
        def load(m, base):
            return near_s[m // 2, pl.ds(k * DOFS + base, 16), m % 2 * AGG : (m % 2 + 1) * AGG]

        return load

    def load_modes(m, base):
        return modes_t[pl.ds(m * DOFS + base, 16), :]

    zero = jnp.zeros((8, AGG), F32)
    for k in range(1 + FACES):
        sums = list(pair_sums(load_near(k), load_modes)) + [zero] * 4
        for entry in range(0, BLOCK, 8):
            diag_s[k, entry : entry + 8] = row_sums(sums[entry : entry + 8])
    for f in range(FACES):
        sums = pair_sums(load_near(f + 1), lambda n, base, f=f: other_s[f, pl.ds(n * DOFS + base, 16), :])
        for entry in range(BLOCK):
            partial_s[f, entry * 8 : entry * 8 + 8] = sums[entry]

    for r in range(4):
        pl.when(valid[r])(ghost_copies[r ^ 1].wait_recv)
    arrived = jnp.concatenate([message_in[r] for r in range(4)], axis=0)
    ghosts = jnp.concatenate([arrived[:, n * DOFS : (n + 1) * DOFS] for n in range(MODES)], axis=0)
    weight_back = plain_dot(arrived[:, WIDTH:].T[:16], select)
    parts = [zero] * 4
    scale = []
    for f in range(FACES):
        target = jnp.broadcast_to(targets[:, f * AGG : (f + 1) * AGG], (8, AGG)) - AGG
        wanted = [iota((8, AGG), 0) + 8 * group == target for group in range(4 * GHOST // 8)]
        for pair in range(MODES // 2):
            product = plain_dot(ghosts, near_s[pair, (f + 1) * DOFS : (f + 2) * DOFS])
            for half in range(2):
                for n in range(MODES):
                    taken = zero
                    for group, mask in enumerate(wanted):
                        at = n * 4 * GHOST + group * 8
                        taken = jnp.where(mask, product[at : at + 8, half * AGG : (half + 1) * AGG], taken)
                    entry = (2 * pair + half) * MODES + n
                    parts.append(partial_s[f, entry * 8 : entry * 8 + 8] + taken)

    total = []
    for f in range(FACES):
        total.append(
            weight[:, f * AGG : (f + 1) * AGG]
            + weight_local[f : f + 1]
            + (weight_back[f : f + 1] + weight_back[f + FACES : f + FACES + 1])
        )
    diag = diag_s[0]
    for f in range(FACES):
        diag = diag + total[f] * diag_s[f + 1]
    faces = jnp.concatenate([row_sums(parts[e : e + 8]) for e in range(0, FACES * BLOCK + 4, 8)], axis=0)
    factor = jnp.concatenate(
        [jnp.zeros((4, AGG), F32)]
        + [jnp.broadcast_to(-weight[:, f * AGG : (f + 1) * AGG], (BLOCK, AGG)) for f in range(FACES)],
        axis=0,
    )
    faces = faces * factor
    coarse_t = jnp.concatenate([diag[:32], diag[32:] + faces[:8], faces[8:]], axis=0)

    first = lanes_dot(place_s[...], coarse_t[:128].astype(BF16)).astype(BF16)
    last = jnp.concatenate([jnp.where(rank == s, coarse_t[128:], 0.0) for s in range(CAP)], axis=0).astype(BF16)
    last = lanes_dot(owned_ones, last)
    send_s[:, :4] = first.reshape(wide_size, 4, 2, 128)
    send_s[:, 4] = jnp.concatenate([last[:, None], jnp.zeros((wide_size, 1, 128), F32)], axis=1).astype(BF16)

    pl.when(jnp.logical_not(is_hub))(lambda: pl.semaphore_wait(everyone, 1))

    def send_rows(i, carry):
        peer = partner(i)
        pltpu.make_async_remote_copy(
            src_ref=send_s.at[peer],
            dst_ref=recv_s.at[w],
            send_sem=row_send,
            recv_sem=row_recv,
            device_id=(g, peer),
            device_id_type=MESH,
        ).start()
        return carry

    lax.fori_loop(0, wide_size - 1, send_rows, 0)
    pltpu.make_async_copy(send_s.at[w], recv_s.at[w], row_recv).start()
    for r in range(4):
        pl.when(valid[r])(ghost_copies[r].wait_send)
    column = iota((wide_size, wide_size * CAP), 1)
    sender = ones_where(column // CAP == iota((wide_size, wide_size * CAP), 0))
    pltpu.make_async_copy(recv_s, recv_s, row_recv).wait()

    out_ref[:128, :] = recv_s[:, :4].reshape(wide_size * CAP, 128).T.astype(F32)
    last = plain_dot(recv_s[:, 4].astype(F32)[:, 0].T.astype(BF16), sender)
    slot = lax.rem(iota((16, wide_size * CAP), 1), CAP)
    tail = jnp.zeros((16, wide_size * CAP), F32)
    for s in range(CAP):
        tail = jnp.where(slot == s, last[s * 16 : (s + 1) * 16], tail)
    out_ref[128:, :] = tail
    sent = send_s.at[pl.ds(0, wide_size - 1)]
    pltpu.make_async_copy(sent, sent, row_send).wait()


def solution(mesh):
    grp_size, wide_size = mesh.shape["grp"], mesh.shape["wide"]

    def shards(null_space, node_damage, face_target, face_damage, ghost_lists, agg_owner, stiffness):
        coarse = pl.pallas_call(
            functools.partial(kernel, grp_size, wide_size),
            out_shape=pltpu.VMEM((ROW, wide_size * CAP), F32),
            in_specs=[pl.BlockSpec(memory_space=pltpu.HBM)] * 7,
            out_specs=pl.BlockSpec(memory_space=pltpu.VMEM),
            scratch_shapes=[
                pltpu.VMEM((AGG, WIDTH), BF16),
                pltpu.VMEM((64, AGG), jnp.int32),
                pltpu.VMEM((FACES, 1, AGG), jnp.int32),
                pltpu.VMEM((FACES, 1, AGG), jnp.int32),
                pltpu.VMEM((4, GHOST), jnp.int32),
                pltpu.VMEM((1, 1, AGG), jnp.int32),
                pltpu.VMEM((DOFS, (1 + FACES) * DOFS), BF16),
                pltpu.VMEM((4, GHOST, MESSAGE), BF16),
                pltpu.VMEM((4, GHOST, MESSAGE), BF16),
                pltpu.VMEM((WIDTH, AGG), BF16),
                pltpu.VMEM(((1 + FACES) * DOFS, DOFS), BF16),
                pltpu.VMEM((MODES // 2, (1 + FACES) * DOFS, 2 * AGG), BF16),
                pltpu.VMEM((FACES, WIDTH, AGG), BF16),
                pltpu.VMEM((1 + FACES, BLOCK + 4, AGG), F32),
                pltpu.VMEM((FACES, BLOCK * 8, AGG), F32),
                pltpu.VMEM((wide_size * CAP, AGG), BF16),
                pltpu.VMEM((wide_size, 5, 2, 128), BF16),
                pltpu.VMEM((wide_size, 5, 2, 128), BF16),
                pltpu.SemaphoreType.DMA((7,)),
                pltpu.SemaphoreType.DMA((4,)),
                pltpu.SemaphoreType.DMA((4,)),
                pltpu.SemaphoreType.DMA,
                pltpu.SemaphoreType.DMA,
                pltpu.SemaphoreType.REGULAR,
            ],
            compiler_params=pltpu.CompilerParams(
                collective_id=0, has_side_effects=True, vmem_limit_bytes=56 * 1024 * 1024
            ),
            cost_estimate=pl.CostEstimate(flops=400_000_000, bytes_accessed=1_000_000, transcendentals=0),
        )(
            null_space[0],
            jnp.transpose(node_damage[0]),
            jnp.transpose(face_target, (2, 0, 1)),
            jnp.transpose(face_damage, (2, 0, 1)),
            ghost_lists[0, 0],
            jnp.transpose(agg_owner, (0, 2, 1)),
            stiffness,
        )
        return coarse[None]

    placed = (
        P("grp", "wide", None),
        P("grp", "wide", None),
        P("grp", "wide", None),
        P("grp", "wide", None),
        P("grp", "wide", None, None),
        P("grp", "wide", None),
        P(),
    )
    return jax.shard_map(
        shards, mesh=mesh, in_specs=placed, out_specs=P("grp", "wide", None), check_vma=False
    )
```

```python
import functools

import jax
import jax.numpy as jnp
from jax import lax
from jax.experimental import pallas as pl
from jax.experimental.pallas import tpu as pltpu
from jax.sharding import PartitionSpec as P

AGG = 128
MODES = 6
DOFS = 192
FACES = 3
LEVELS = 8
GHOST = 16
CAP = 8
WIDTH = MODES * DOFS
BLOCK = MODES * MODES
ROW = (1 + FACES) * BLOCK
MESSAGE = WIDTH + 128
MESH = pl.DeviceIdType.MESH
F32 = jnp.float32
BF16 = jnp.bfloat16


def lanes_dot(left, right):
    return lax.dot_general(left, right, (((1,), (1,)), ((), ())), preferred_element_type=F32)


def plain_dot(left, right):
    return jnp.dot(left, right, preferred_element_type=F32)


def ones_where(condition):
    return jnp.where(condition, 1.0, 0.0).astype(BF16)


def iota(shape, dim):
    return lax.broadcasted_iota(jnp.int32, shape, dim)


def pair_sums(load_left, load_right):
    def step(i, sums):
        base = pl.multiple_of(i * 16, 16)
        left = [load_left(m, base).astype(F32) for m in range(MODES)]
        right = [load_right(n, base).astype(F32) for n in range(MODES)]
        new = []
        for m in range(MODES):
            for n in range(MODES):
                product = left[m] * right[n]
                new.append(sums[m * MODES + n] + (product[:8] + product[8:]))
        return tuple(new)

    zero = jnp.zeros((8, AGG), F32)
    return lax.fori_loop(0, DOFS // 16, step, (zero,) * BLOCK, unroll=True)


def row_sums(parts):
    sub = iota((8, AGG), 0)

    def halves(low, high, bit):
        low = low + pltpu.roll(low, 8 - bit, 0)
        high = high + pltpu.roll(high, bit, 0)
        return jnp.where((sub & bit) == 0, low, high)

    for bit in (4, 2, 1):
        count = len(parts) // 2
        parts = [halves(parts[i], parts[i + count], bit) for i in range(count)]
    return parts[0]


def kernel(
    grp_size, wide_size,
    null_hbm, damage_hbm, target_hbm, face_hbm, list_hbm, owner_hbm, stiff_hbm,
    out_ref,
    null_v, damage_v, target_v, face_v, list_v, owner_v, stiff_v,
    message_out, message_in, modes_t, stiff_t, near_s, other_s, diag_s, partial_s, place_s, send_s, recv_s,
    in_sem, ghost_send, ghost_recv, row_send, row_recv, everyone,
):
    g = lax.axis_index("grp")
    w = lax.axis_index("wide")

    barrier = pltpu.get_barrier_semaphore()
    neighbours = [(g - 1, w), (g + 1, w), (g, w - 1), (g, w + 1)]
    valid = [g > 0, g < grp_size - 1, w > 0, w < wide_size - 1]
    hub = wide_size * 23 // 32
    is_hub = w == hub

    def greet(peer, condition):
        @pl.when(condition)
        def _():
            pl.semaphore_signal(barrier, inc=1, device_id=peer, device_id_type=MESH)

    for peer, condition in zip(neighbours, valid):
        greet(peer, condition)
    greet((g, hub), w != hub)

    loads = [
        pltpu.make_async_copy(source, target, in_sem.at[k])
        for k, (source, target) in enumerate(
            [
                (list_hbm, list_v), (damage_hbm, damage_v), (null_hbm, null_v), (target_hbm, target_v),
                (face_hbm, face_v), (owner_hbm, owner_v), (stiff_hbm, stiff_v),
            ]
        )
    ]
    for load in loads:
        load.start()

    loads[0].wait()
    listed = list_v[...].astype(F32)
    spread = jnp.concatenate([jnp.broadcast_to(listed[r : r + 1], (GHOST, GHOST)) for r in range(4)], axis=0)
    on_diagonal = (iota((4 * GHOST, GHOST), 0) & (GHOST - 1)) == iota((4 * GHOST, GHOST), 1)
    list_column = jnp.sum(jnp.where(on_diagonal, spread, 0.0), axis=1, keepdims=True).astype(jnp.int32)
    select = ones_where(list_column == iota((4 * GHOST, AGG), 1))

    loads[1].wait()
    levels = ((LEVELS - damage_v[...]).astype(F32) * (1.0 / LEVELS)).T.astype(BF16)
    node_of = ((iota((1, WIDTH), 1) * 43691) >> 17) & 63
    widen = ones_where(iota((64, WIDTH), 0) == node_of)
    scales = plain_dot(levels, widen)
    loads[2].wait()
    modes = (null_v[...].astype(F32) * scales).astype(BF16)
    picked = plain_dot(select, modes).astype(BF16)

    loads[3].wait()
    loads[4].wait()
    targets = jnp.concatenate([target_v[f] for f in range(FACES)], axis=1)
    levels_f = jnp.concatenate([face_v[f] for f in range(FACES)], axis=1)
    level = (LEVELS - levels_f).astype(F32) * (1.0 / LEVELS)
    weight = level * level
    chosen = ones_where(iota((AGG + 4 * GHOST, FACES * AGG), 0) == targets)
    row = iota((AGG, FACES * AGG), 0)
    face_of = iota((AGG, FACES * AGG), 1) >> 7
    weight_rows = jnp.where((row == face_of) | (row == face_of + FACES), weight, 0.0).astype(BF16)
    weight_local = lanes_dot(weight_rows[:16], chosen[:AGG])
    weight_ghost = lanes_dot(chosen[AGG:], weight_rows)
    high = weight_ghost.astype(BF16).astype(F32)
    split = jnp.where(iota((4 * GHOST, 128), 1) < FACES, high, weight_ghost - high).astype(BF16)
    for r in range(4):
        message_out[r, :, :WIDTH] = picked[r * GHOST : (r + 1) * GHOST]
        message_out[r, :, WIDTH:] = split[r * GHOST : (r + 1) * GHOST]

    for r in range(4):
        @pl.when(jnp.logical_not(valid[r]))
        def _(r=r):
            message_in[r] = jnp.zeros((GHOST, MESSAGE), BF16)

    near_count = sum(condition.astype(jnp.int32) for condition in valid)
    pl.semaphore_wait(barrier, near_count + is_hub.astype(jnp.int32) * (wide_size - 1))
    ghost_copies = [
        pltpu.make_async_remote_copy(
            src_ref=message_out.at[r],
            dst_ref=message_in.at[r ^ 1],
            send_sem=ghost_send.at[r],
            recv_sem=ghost_recv.at[r ^ 1],
            device_id=neighbours[r],
            device_id_type=MESH,
        )
        for r in range(4)
    ]
    for r in range(4):
        pl.when(valid[r])(ghost_copies[r].start)

    @pl.when(is_hub)
    def _():
        def tell(i, carry):
            step = i // 2 + 1
            peer = lax.rem(w + step + lax.rem(i, 2) * (wide_size - 2 * step), wide_size)
            pl.semaphore_signal(everyone, inc=1, device_id=(g, peer), device_id_type=MESH)
            return carry

        lax.fori_loop(0, wide_size - 1, tell, 0)

    modes_t[...] = modes.T
    loads[6].wait()
    stiff_t[...] = stiff_v[...].T
    for pair in range(MODES // 2):
        two = jnp.concatenate(
            [modes_t[(2 * pair + h) * DOFS : (2 * pair + h + 1) * DOFS] for h in range(2)], axis=1
        )
        near_s[pair] = plain_dot(stiff_t[...], two).astype(BF16)
    for f in range(FACES):
        other_s[f] = plain_dot(modes_t[...], chosen[:AGG, f * AGG : (f + 1) * AGG]).astype(BF16)

    loads[5].wait()
    owner = owner_v[0]
    owned = iota((wide_size, AGG), 0) == owner
    owned_ones = ones_where(owned)
    before = ones_where(iota((AGG, AGG), 0) < iota((AGG, AGG), 1))
    earlier = plain_dot(owned_ones, before)
    rank = jnp.sum(jnp.where(owned, earlier, 0.0), axis=0, keepdims=True).astype(jnp.int32)
    place_s[...] = ones_where(iota((wide_size * CAP, AGG), 0) == owner * CAP + rank)

    def load_near(k):
        def load(m, base):
            return near_s[m // 2, pl.ds(k * DOFS + base, 16), m % 2 * AGG : (m % 2 + 1) * AGG]

        return load

    def load_modes(m, base):
        return modes_t[pl.ds(m * DOFS + base, 16), :]

    zero = jnp.zeros((8, AGG), F32)
    for k in range(1 + FACES):
        sums = list(pair_sums(load_near(k), load_modes)) + [zero] * 4
        for entry in range(0, BLOCK, 8):
            diag_s[k, entry : entry + 8] = row_sums(sums[entry : entry + 8])
    for f in range(FACES):
        sums = pair_sums(load_near(f + 1), lambda n, base, f=f: other_s[f, pl.ds(n * DOFS + base, 16), :])
        for entry in range(BLOCK):
            partial_s[f, entry * 8 : entry * 8 + 8] = sums[entry]

    for r in range(4):
        pl.when(valid[r])(ghost_copies[r ^ 1].wait_recv)
    arrived = jnp.concatenate([message_in[r] for r in range(4)], axis=0)
    ghosts = jnp.concatenate([arrived[:, n * DOFS : (n + 1) * DOFS] for n in range(MODES)], axis=0)
    weight_back = plain_dot(arrived[:, WIDTH:].T[:16], select)
    parts = [zero] * 4
    scale = []
    for f in range(FACES):
        target = jnp.broadcast_to(targets[:, f * AGG : (f + 1) * AGG], (8, AGG)) - AGG
        wanted = [iota((8, AGG), 0) + 8 * group == target for group in range(4 * GHOST // 8)]
        for pair in range(MODES // 2):
            product = plain_dot(ghosts, near_s[pair, (f + 1) * DOFS : (f + 2) * DOFS])
            for half in range(2):
                for n in range(MODES):
                    taken = zero
                    for group, mask in enumerate(wanted):
                        at = n * 4 * GHOST + group * 8
                        taken = jnp.where(mask, product[at : at + 8, half * AGG : (half + 1) * AGG], taken)
                    entry = (2 * pair + half) * MODES + n
                    parts.append(partial_s[f, entry * 8 : entry * 8 + 8] + taken)

    total = []
    for f in range(FACES):
        total.append(
            weight[:, f * AGG : (f + 1) * AGG]
            + weight_local[f : f + 1]
            + (weight_back[f : f + 1] + weight_back[f + FACES : f + FACES + 1])
        )
    diag = diag_s[0]
    for f in range(FACES):
        diag = diag + total[f] * diag_s[f + 1]
    faces = jnp.concatenate([row_sums(parts[e : e + 8]) for e in range(0, FACES * BLOCK + 4, 8)], axis=0)
    factor = jnp.concatenate(
        [jnp.zeros((4, AGG), F32)]
        + [jnp.broadcast_to(-weight[:, f * AGG : (f + 1) * AGG], (BLOCK, AGG)) for f in range(FACES)],
        axis=0,
    )
    faces = faces * factor
    coarse_t = jnp.concatenate([diag[:32], diag[32:] + faces[:8], faces[8:]], axis=0)

    first = lanes_dot(place_s[...], coarse_t[:128].astype(BF16)).astype(BF16)
    last = jnp.concatenate([jnp.where(rank == s, coarse_t[128:], 0.0) for s in range(CAP)], axis=0).astype(BF16)
    last = lanes_dot(owned_ones, last)
    send_s[:, :4] = first.reshape(wide_size, 4, 2, 128)
    send_s[:, 4] = jnp.concatenate([last[:, None], jnp.zeros((wide_size, 1, 128), F32)], axis=1).astype(BF16)

    pl.when(jnp.logical_not(is_hub))(lambda: pl.semaphore_wait(everyone, 1))

    def send_rows(i, carry):
        place = i + (i >= w + 1 - 2 * lax.rem(w, 2)).astype(jnp.int32)
        peer = place + 1 - 2 * lax.rem(place, 2)
        pltpu.make_async_remote_copy(
            src_ref=send_s.at[peer],
            dst_ref=recv_s.at[w],
            send_sem=row_send,
            recv_sem=row_recv.at[w // (wide_size // 2)],
            device_id=(g, peer),
            device_id_type=MESH,
        ).start()
        return carry

    lax.fori_loop(0, wide_size - 1, send_rows, 0)
    half = wide_size // 2
    pltpu.make_async_copy(send_s.at[w], recv_s.at[w], row_recv.at[w // half]).start()
    for r in range(4):
        pl.when(valid[r])(ghost_copies[r].wait_send)
    columns = half * CAP
    column = iota((half, columns), 1)
    sender = ones_where(column // CAP == iota((half, columns), 0))
    slot = lax.rem(iota((16, columns), 1), CAP)
    for part in range(2):
        rows = recv_s.at[pl.ds(part * half, half)]
        at = slice(part * columns, (part + 1) * columns)
        pltpu.make_async_copy(rows, rows, row_recv.at[part]).wait()
        out_ref[:128, at] = rows[:, :4].reshape(columns, 128).T.astype(F32)
        last = plain_dot(rows[:, 4].astype(F32)[:, 0].T.astype(BF16), sender)
        tail = jnp.zeros((16, columns), F32)
        for s in range(CAP):
            tail = jnp.where(slot == s, last[s * 16 : (s + 1) * 16], tail)
        out_ref[128:, at] = tail
    sent = send_s.at[pl.ds(0, wide_size - 1)]
    pltpu.make_async_copy(sent, sent, row_send).wait()


def solution(mesh):
    grp_size, wide_size = mesh.shape["grp"], mesh.shape["wide"]

    def shards(null_space, node_damage, face_target, face_damage, ghost_lists, agg_owner, stiffness):
        coarse = pl.pallas_call(
            functools.partial(kernel, grp_size, wide_size),
            out_shape=pltpu.VMEM((ROW, wide_size * CAP), F32),
            in_specs=[pl.BlockSpec(memory_space=pltpu.HBM)] * 7,
            out_specs=pl.BlockSpec(memory_space=pltpu.VMEM),
            scratch_shapes=[
                pltpu.VMEM((AGG, WIDTH), BF16),
                pltpu.VMEM((64, AGG), jnp.int32),
                pltpu.VMEM((FACES, 1, AGG), jnp.int32),
                pltpu.VMEM((FACES, 1, AGG), jnp.int32),
                pltpu.VMEM((4, GHOST), jnp.int32),
                pltpu.VMEM((1, 1, AGG), jnp.int32),
                pltpu.VMEM((DOFS, (1 + FACES) * DOFS), BF16),
                pltpu.VMEM((4, GHOST, MESSAGE), BF16),
                pltpu.VMEM((4, GHOST, MESSAGE), BF16),
                pltpu.VMEM((WIDTH, AGG), BF16),
                pltpu.VMEM(((1 + FACES) * DOFS, DOFS), BF16),
                pltpu.VMEM((MODES // 2, (1 + FACES) * DOFS, 2 * AGG), BF16),
                pltpu.VMEM((FACES, WIDTH, AGG), BF16),
                pltpu.VMEM((1 + FACES, BLOCK + 4, AGG), F32),
                pltpu.VMEM((FACES, BLOCK * 8, AGG), F32),
                pltpu.VMEM((wide_size * CAP, AGG), BF16),
                pltpu.VMEM((wide_size, 5, 2, 128), BF16),
                pltpu.VMEM((wide_size, 5, 2, 128), BF16),
                pltpu.SemaphoreType.DMA((7,)),
                pltpu.SemaphoreType.DMA((4,)),
                pltpu.SemaphoreType.DMA((4,)),
                pltpu.SemaphoreType.DMA,
                pltpu.SemaphoreType.DMA((2,)),
                pltpu.SemaphoreType.REGULAR,
            ],
            compiler_params=pltpu.CompilerParams(
                collective_id=0, has_side_effects=True, vmem_limit_bytes=56 * 1024 * 1024
            ),
            cost_estimate=pl.CostEstimate(flops=400_000_000, bytes_accessed=1_000_000, transcendentals=0),
        )(
            null_space[0],
            jnp.transpose(node_damage[0]),
            jnp.transpose(face_target, (2, 0, 1)),
            jnp.transpose(face_damage, (2, 0, 1)),
            ghost_lists[0, 0],
            jnp.transpose(agg_owner, (0, 2, 1)),
            stiffness,
        )
        return coarse[None]

    placed = (
        P("grp", "wide", None),
        P("grp", "wide", None),
        P("grp", "wide", None),
        P("grp", "wide", None),
        P("grp", "wide", None, None),
        P("grp", "wide", None),
        P(),
    )
    return jax.shard_map(
        shards, mesh=mesh, in_specs=placed, out_specs=P("grp", "wide", None), check_vma=False
    )
```

```python
import functools

import jax
import jax.numpy as jnp
from jax import lax
from jax.experimental import pallas as pl
from jax.experimental.pallas import tpu as pltpu
from jax.sharding import PartitionSpec as P

AGG = 128
MODES = 6
DOFS = 192
FACES = 3
LEVELS = 8
GHOST = 16
CAP = 8
WIDTH = MODES * DOFS
BLOCK = MODES * MODES
ROW = (1 + FACES) * BLOCK
MESSAGE = WIDTH + 128
MESH = pl.DeviceIdType.MESH
F32 = jnp.float32
BF16 = jnp.bfloat16


def lanes_dot(left, right):
    return lax.dot_general(left, right, (((1,), (1,)), ((), ())), preferred_element_type=F32)


def plain_dot(left, right):
    return jnp.dot(left, right, preferred_element_type=F32)


def ones_where(condition):
    return jnp.where(condition, 1.0, 0.0).astype(BF16)


def iota(shape, dim):
    return lax.broadcasted_iota(jnp.int32, shape, dim)


def pair_sums(load_left, load_right):
    def step(i, sums):
        base = pl.multiple_of(i * 16, 16)
        left = [load_left(m, base).astype(F32) for m in range(MODES)]
        right = [load_right(n, base).astype(F32) for n in range(MODES)]
        new = []
        for m in range(MODES):
            for n in range(MODES):
                product = left[m] * right[n]
                new.append(sums[m * MODES + n] + (product[:8] + product[8:]))
        return tuple(new)

    zero = jnp.zeros((8, AGG), F32)
    return lax.fori_loop(0, DOFS // 16, step, (zero,) * BLOCK, unroll=True)


def row_sums(parts):
    sub = iota((8, AGG), 0)

    def halves(low, high, bit):
        low = low + pltpu.roll(low, 8 - bit, 0)
        high = high + pltpu.roll(high, bit, 0)
        return jnp.where((sub & bit) == 0, low, high)

    for bit in (4, 2, 1):
        count = len(parts) // 2
        parts = [halves(parts[i], parts[i + count], bit) for i in range(count)]
    return parts[0]


def kernel(
    grp_size, wide_size,
    null_hbm, damage_hbm, target_hbm, face_hbm, list_hbm, owner_hbm, stiff_hbm,
    out_ref,
    null_v, damage_v, target_v, face_v, list_v, owner_v, stiff_v,
    message_out, message_in, modes_t, stiff_t, near_s, other_s, diag_s, partial_s, place_s, send_s, recv_s,
    in_sem, ghost_send, ghost_recv, row_send, row_recv, everyone,
):
    g = lax.axis_index("grp")
    w = lax.axis_index("wide")

    barrier = pltpu.get_barrier_semaphore()
    neighbours = [(g - 1, w), (g + 1, w), (g, w - 1), (g, w + 1)]
    valid = [g > 0, g < grp_size - 1, w > 0, w < wide_size - 1]
    hub = wide_size * 21 // 32
    is_hub = w == hub

    def greet(peer, condition):
        @pl.when(condition)
        def _():
            pl.semaphore_signal(barrier, inc=1, device_id=peer, device_id_type=MESH)

    for peer, condition in zip(neighbours, valid):
        greet(peer, condition)
    greet((g, hub), w != hub)

    loads = [
        pltpu.make_async_copy(source, target, in_sem.at[k])
        for k, (source, target) in enumerate(
            [
                (list_hbm, list_v), (damage_hbm, damage_v), (null_hbm, null_v), (target_hbm, target_v),
                (face_hbm, face_v), (owner_hbm, owner_v), (stiff_hbm, stiff_v),
            ]
        )
    ]
    for load in loads:
        load.start()

    loads[0].wait()
    listed = list_v[...].astype(F32)
    spread = jnp.concatenate([jnp.broadcast_to(listed[r : r + 1], (GHOST, GHOST)) for r in range(4)], axis=0)
    on_diagonal = (iota((4 * GHOST, GHOST), 0) & (GHOST - 1)) == iota((4 * GHOST, GHOST), 1)
    list_column = jnp.sum(jnp.where(on_diagonal, spread, 0.0), axis=1, keepdims=True).astype(jnp.int32)
    select = ones_where(list_column == iota((4 * GHOST, AGG), 1))

    loads[1].wait()
    levels = ((LEVELS - damage_v[...]).astype(F32) * (1.0 / LEVELS)).T.astype(BF16)
    node_of = ((iota((1, WIDTH), 1) * 43691) >> 17) & 63
    widen = ones_where(iota((64, WIDTH), 0) == node_of)
    scales = plain_dot(levels, widen)
    loads[2].wait()
    modes = (null_v[...].astype(F32) * scales).astype(BF16)
    picked = plain_dot(select, modes).astype(BF16)

    loads[3].wait()
    loads[4].wait()
    targets = jnp.concatenate([target_v[f] for f in range(FACES)], axis=1)
    levels_f = jnp.concatenate([face_v[f] for f in range(FACES)], axis=1)
    level = (LEVELS - levels_f).astype(F32) * (1.0 / LEVELS)
    weight = level * level
    chosen = ones_where(iota((AGG + 4 * GHOST, FACES * AGG), 0) == targets)
    row = iota((AGG, FACES * AGG), 0)
    face_of = iota((AGG, FACES * AGG), 1) >> 7
    weight_rows = jnp.where((row == face_of) | (row == face_of + FACES), weight, 0.0).astype(BF16)
    weight_local = lanes_dot(weight_rows[:16], chosen[:AGG])
    weight_ghost = lanes_dot(chosen[AGG:], weight_rows)
    high = weight_ghost.astype(BF16).astype(F32)
    split = jnp.where(iota((4 * GHOST, 128), 1) < FACES, high, weight_ghost - high).astype(BF16)
    for r in range(4):
        message_out[r, :, :WIDTH] = picked[r * GHOST : (r + 1) * GHOST]
        message_out[r, :, WIDTH:] = split[r * GHOST : (r + 1) * GHOST]

    for r in range(4):
        @pl.when(jnp.logical_not(valid[r]))
        def _(r=r):
            message_in[r] = jnp.zeros((GHOST, MESSAGE), BF16)

    near_count = sum(condition.astype(jnp.int32) for condition in valid)
    pl.semaphore_wait(barrier, near_count + is_hub.astype(jnp.int32) * (wide_size - 1))
    ghost_copies = [
        pltpu.make_async_remote_copy(
            src_ref=message_out.at[r],
            dst_ref=message_in.at[r ^ 1],
            send_sem=ghost_send.at[r],
            recv_sem=ghost_recv.at[r ^ 1],
            device_id=neighbours[r],
            device_id_type=MESH,
        )
        for r in range(4)
    ]
    for r in (2, 3, 1, 0):
        pl.when(valid[r])(ghost_copies[r].start)

    @pl.when(is_hub)
    def _():
        def tell(i, carry):
            step = i // 2 + 1
            peer = lax.rem(w + step + lax.rem(i, 2) * (wide_size - 2 * step), wide_size)
            pl.semaphore_signal(everyone, inc=1, device_id=(g, peer), device_id_type=MESH)
            return carry

        lax.fori_loop(0, wide_size - 1, tell, 0)

    modes_t[...] = modes.T
    loads[6].wait()
    stiff_t[...] = stiff_v[...].T
    for pair in range(MODES // 2):
        two = jnp.concatenate(
            [modes_t[(2 * pair + h) * DOFS : (2 * pair + h + 1) * DOFS] for h in range(2)], axis=1
        )
        near_s[pair] = plain_dot(stiff_t[...], two).astype(BF16)
    for f in range(FACES):
        other_s[f] = plain_dot(modes_t[...], chosen[:AGG, f * AGG : (f + 1) * AGG]).astype(BF16)

    loads[5].wait()
    owner = owner_v[0]
    owned = iota((wide_size, AGG), 0) == owner
    owned_ones = ones_where(owned)
    before = ones_where(iota((AGG, AGG), 0) < iota((AGG, AGG), 1))
    earlier = plain_dot(owned_ones, before)
    rank = jnp.sum(jnp.where(owned, earlier, 0.0), axis=0, keepdims=True).astype(jnp.int32)
    place_s[...] = ones_where(iota((wide_size * CAP, AGG), 0) == owner * CAP + rank)

    def load_near(k):
        def load(m, base):
            return near_s[m // 2, pl.ds(k * DOFS + base, 16), m % 2 * AGG : (m % 2 + 1) * AGG]

        return load

    def load_modes(m, base):
        return modes_t[pl.ds(m * DOFS + base, 16), :]

    zero = jnp.zeros((8, AGG), F32)
    for k in range(1 + FACES):
        sums = list(pair_sums(load_near(k), load_modes)) + [zero] * 4
        for entry in range(0, BLOCK, 8):
            diag_s[k, entry : entry + 8] = row_sums(sums[entry : entry + 8])
    for f in range(FACES):
        sums = pair_sums(load_near(f + 1), lambda n, base, f=f: other_s[f, pl.ds(n * DOFS + base, 16), :])
        for entry in range(BLOCK):
            partial_s[f, entry * 8 : entry * 8 + 8] = sums[entry]

    for r in range(4):
        pl.when(valid[r])(ghost_copies[r ^ 1].wait_recv)
    arrived = jnp.concatenate([message_in[r] for r in range(4)], axis=0)
    ghosts = jnp.concatenate([arrived[:, n * DOFS : (n + 1) * DOFS] for n in range(MODES)], axis=0)
    weight_back = plain_dot(arrived[:, WIDTH:].T[:16], select)
    parts = [zero] * 4
    scale = []
    for f in range(FACES):
        target = jnp.broadcast_to(targets[:, f * AGG : (f + 1) * AGG], (8, AGG)) - AGG
        wanted = [iota((8, AGG), 0) + 8 * group == target for group in range(4 * GHOST // 8)]
        for pair in range(MODES // 2):
            product = plain_dot(ghosts, near_s[pair, (f + 1) * DOFS : (f + 2) * DOFS])
            for half in range(2):
                for n in range(MODES):
                    taken = zero
                    for group, mask in enumerate(wanted):
                        at = n * 4 * GHOST + group * 8
                        taken = jnp.where(mask, product[at : at + 8, half * AGG : (half + 1) * AGG], taken)
                    entry = (2 * pair + half) * MODES + n
                    parts.append(partial_s[f, entry * 8 : entry * 8 + 8] + taken)

    total = []
    for f in range(FACES):
        total.append(
            weight[:, f * AGG : (f + 1) * AGG]
            + weight_local[f : f + 1]
            + (weight_back[f : f + 1] + weight_back[f + FACES : f + FACES + 1])
        )
    diag = diag_s[0]
    for f in range(FACES):
        diag = diag + total[f] * diag_s[f + 1]
    faces = jnp.concatenate([row_sums(parts[e : e + 8]) for e in range(0, FACES * BLOCK + 4, 8)], axis=0)
    factor = jnp.concatenate(
        [jnp.zeros((4, AGG), F32)]
        + [jnp.broadcast_to(-weight[:, f * AGG : (f + 1) * AGG], (BLOCK, AGG)) for f in range(FACES)],
        axis=0,
    )
    faces = faces * factor
    coarse_t = jnp.concatenate([diag[:32], diag[32:] + faces[:8], faces[8:]], axis=0)

    first = lanes_dot(place_s[...], coarse_t[:128].astype(BF16)).astype(BF16)
    last = jnp.concatenate([jnp.where(rank == s, coarse_t[128:], 0.0) for s in range(CAP)], axis=0).astype(BF16)
    last = lanes_dot(owned_ones, last)
    send_s[:, :4] = first.reshape(wide_size, 4, 2, 128)
    send_s[:, 4] = jnp.concatenate([last[:, None], jnp.zeros((wide_size, 1, 128), F32)], axis=1).astype(BF16)

    pl.when(jnp.logical_not(is_hub))(lambda: pl.semaphore_wait(everyone, 1))

    def send_rows(i, carry):
        place = i + (i >= w + 1 - 2 * lax.rem(w, 2)).astype(jnp.int32)
        peer = place + 1 - 2 * lax.rem(place, 2)
        pltpu.make_async_remote_copy(
            src_ref=send_s.at[peer],
            dst_ref=recv_s.at[w],
            send_sem=row_send,
            recv_sem=row_recv.at[w // (wide_size // 2)],
            device_id=(g, peer),
            device_id_type=MESH,
        ).start()
        return carry

    lax.fori_loop(0, wide_size - 1, send_rows, 0)
    half = wide_size // 2
    pltpu.make_async_copy(send_s.at[w], recv_s.at[w], row_recv.at[w // half]).start()
    for r in range(4):
        pl.when(valid[r])(ghost_copies[r].wait_send)
    columns = half * CAP
    column = iota((half, columns), 1)
    sender = ones_where(column // CAP == iota((half, columns), 0))
    slot = lax.rem(iota((16, columns), 1), CAP)
    for part in range(2):
        rows = recv_s.at[pl.ds(part * half, half)]
        at = slice(part * columns, (part + 1) * columns)
        pltpu.make_async_copy(rows, rows, row_recv.at[part]).wait()
        out_ref[:128, at] = rows[:, :4].reshape(columns, 128).T.astype(F32)
        last = plain_dot(rows[:, 4].astype(F32)[:, 0].T.astype(BF16), sender)
        tail = jnp.zeros((16, columns), F32)
        for s in range(CAP):
            tail = jnp.where(slot == s, last[s * 16 : (s + 1) * 16], tail)
        out_ref[128:, at] = tail
    sent = send_s.at[pl.ds(0, wide_size - 1)]
    pltpu.make_async_copy(sent, sent, row_send).wait()


def solution(mesh):
    grp_size, wide_size = mesh.shape["grp"], mesh.shape["wide"]

    def shards(null_space, node_damage, face_target, face_damage, ghost_lists, agg_owner, stiffness):
        coarse = pl.pallas_call(
            functools.partial(kernel, grp_size, wide_size),
            out_shape=pltpu.VMEM((ROW, wide_size * CAP), F32),
            in_specs=[pl.BlockSpec(memory_space=pltpu.HBM)] * 7,
            out_specs=pl.BlockSpec(memory_space=pltpu.VMEM),
            scratch_shapes=[
                pltpu.VMEM((AGG, WIDTH), BF16),
                pltpu.VMEM((64, AGG), jnp.int32),
                pltpu.VMEM((FACES, 1, AGG), jnp.int32),
                pltpu.VMEM((FACES, 1, AGG), jnp.int32),
                pltpu.VMEM((4, GHOST), jnp.int32),
                pltpu.VMEM((1, 1, AGG), jnp.int32),
                pltpu.VMEM((DOFS, (1 + FACES) * DOFS), BF16),
                pltpu.VMEM((4, GHOST, MESSAGE), BF16),
                pltpu.VMEM((4, GHOST, MESSAGE), BF16),
                pltpu.VMEM((WIDTH, AGG), BF16),
                pltpu.VMEM(((1 + FACES) * DOFS, DOFS), BF16),
                pltpu.VMEM((MODES // 2, (1 + FACES) * DOFS, 2 * AGG), BF16),
                pltpu.VMEM((FACES, WIDTH, AGG), BF16),
                pltpu.VMEM((1 + FACES, BLOCK + 4, AGG), F32),
                pltpu.VMEM((FACES, BLOCK * 8, AGG), F32),
                pltpu.VMEM((wide_size * CAP, AGG), BF16),
                pltpu.VMEM((wide_size, 5, 2, 128), BF16),
                pltpu.VMEM((wide_size, 5, 2, 128), BF16),
                pltpu.SemaphoreType.DMA((7,)),
                pltpu.SemaphoreType.DMA((4,)),
                pltpu.SemaphoreType.DMA((4,)),
                pltpu.SemaphoreType.DMA,
                pltpu.SemaphoreType.DMA((2,)),
                pltpu.SemaphoreType.REGULAR,
            ],
            compiler_params=pltpu.CompilerParams(
                collective_id=0, has_side_effects=True, vmem_limit_bytes=56 * 1024 * 1024
            ),
            cost_estimate=pl.CostEstimate(flops=400_000_000, bytes_accessed=1_000_000, transcendentals=0),
        )(
            null_space[0],
            jnp.transpose(node_damage[0]),
            jnp.transpose(face_target, (2, 0, 1)),
            jnp.transpose(face_damage, (2, 0, 1)),
            ghost_lists[0, 0],
            jnp.transpose(agg_owner, (0, 2, 1)),
            stiffness,
        )
        return coarse[None]

    placed = (
        P("grp", "wide", None),
        P("grp", "wide", None),
        P("grp", "wide", None),
        P("grp", "wide", None),
        P("grp", "wide", None, None),
        P("grp", "wide", None),
        P(),
    )
    return jax.shard_map(
        shards, mesh=mesh, in_specs=placed, out_specs=P("grp", "wide", None), check_vma=False
    )
```

```python
import functools

import jax
import jax.numpy as jnp
from jax import lax
from jax.experimental import pallas as pl
from jax.experimental.pallas import tpu as pltpu
from jax.sharding import PartitionSpec as P

AGG = 128
MODES = 6
DOFS = 192
FACES = 3
LEVELS = 8
GHOST = 16
CAP = 8
WIDTH = MODES * DOFS
BLOCK = MODES * MODES
ROW = (1 + FACES) * BLOCK
MESSAGE = WIDTH + 128
MESH = pl.DeviceIdType.MESH
F32 = jnp.float32
BF16 = jnp.bfloat16


def lanes_dot(left, right):
    return lax.dot_general(left, right, (((1,), (1,)), ((), ())), preferred_element_type=F32)


def plain_dot(left, right):
    return jnp.dot(left, right, preferred_element_type=F32)


def ones_where(condition):
    return jnp.where(condition, 1.0, 0.0).astype(BF16)


def iota(shape, dim):
    return lax.broadcasted_iota(jnp.int32, shape, dim)


def pair_sums(load_left, load_right):
    def step(i, sums):
        base = pl.multiple_of(i * 16, 16)
        left = [load_left(m, base).astype(F32) for m in range(MODES)]
        right = [load_right(n, base).astype(F32) for n in range(MODES)]
        new = []
        for m in range(MODES):
            for n in range(MODES):
                product = left[m] * right[n]
                new.append(sums[m * MODES + n] + (product[:8] + product[8:]))
        return tuple(new)

    zero = jnp.zeros((8, AGG), F32)
    return lax.fori_loop(0, DOFS // 16, step, (zero,) * BLOCK, unroll=True)


def row_sums(parts):
    sub = iota((8, AGG), 0)

    def halves(low, high, bit):
        low = low + pltpu.roll(low, 8 - bit, 0)
        high = high + pltpu.roll(high, bit, 0)
        return jnp.where((sub & bit) == 0, low, high)

    for bit in (4, 2, 1):
        count = len(parts) // 2
        parts = [halves(parts[i], parts[i + count], bit) for i in range(count)]
    return parts[0]


def kernel(
    grp_size, wide_size,
    null_hbm, damage_hbm, target_hbm, face_hbm, list_hbm, owner_hbm, stiff_hbm,
    out_ref,
    null_v, damage_v, target_v, face_v, list_v, owner_v, stiff_v,
    message_out, message_in, modes_t, stiff_t, near_s, other_s, diag_s, partial_s, place_s, send_s, recv_s,
    in_sem, ghost_send, ghost_recv, row_send, row_recv, everyone,
):
    g = lax.axis_index("grp")
    w = lax.axis_index("wide")

    barrier = pltpu.get_barrier_semaphore()
    neighbours = [(g - 1, w), (g + 1, w), (g, w - 1), (g, w + 1)]
    valid = [g > 0, g < grp_size - 1, w > 0, w < wide_size - 1]
    hub = wide_size * 23 // 32
    is_hub = w == hub

    def greet(peer, condition):
        @pl.when(condition)
        def _():
            pl.semaphore_signal(barrier, inc=1, device_id=peer, device_id_type=MESH)

    for peer, condition in zip(neighbours, valid):
        greet(peer, condition)
    greet((g, hub), w != hub)

    loads = [
        pltpu.make_async_copy(source, target, in_sem.at[k])
        for k, (source, target) in enumerate(
            [
                (list_hbm, list_v), (damage_hbm, damage_v), (null_hbm, null_v), (target_hbm, target_v),
                (face_hbm, face_v), (owner_hbm, owner_v), (stiff_hbm, stiff_v),
            ]
        )
    ]
    for load in loads:
        load.start()

    loads[0].wait()
    listed = list_v[...].astype(F32)
    spread = jnp.concatenate([jnp.broadcast_to(listed[r : r + 1], (GHOST, GHOST)) for r in range(4)], axis=0)
    on_diagonal = (iota((4 * GHOST, GHOST), 0) & (GHOST - 1)) == iota((4 * GHOST, GHOST), 1)
    list_column = jnp.sum(jnp.where(on_diagonal, spread, 0.0), axis=1, keepdims=True).astype(jnp.int32)
    select = ones_where(list_column == iota((4 * GHOST, AGG), 1))

    loads[1].wait()
    levels = ((LEVELS - damage_v[...]).astype(F32) * (1.0 / LEVELS)).T.astype(BF16)
    node_of = ((iota((1, WIDTH), 1) * 43691) >> 17) & 63
    widen = ones_where(iota((64, WIDTH), 0) == node_of)
    scales = plain_dot(levels, widen)
    loads[2].wait()
    modes = (null_v[...].astype(F32) * scales).astype(BF16)
    picked = plain_dot(select, modes).astype(BF16)

    loads[3].wait()
    loads[4].wait()
    targets = jnp.concatenate([target_v[f] for f in range(FACES)], axis=1)
    levels_f = jnp.concatenate([face_v[f] for f in range(FACES)], axis=1)
    level = (LEVELS - levels_f).astype(F32) * (1.0 / LEVELS)
    weight = level * level
    chosen = ones_where(iota((AGG + 4 * GHOST, FACES * AGG), 0) == targets)
    row = iota((AGG, FACES * AGG), 0)
    face_of = iota((AGG, FACES * AGG), 1) >> 7
    weight_rows = jnp.where((row == face_of) | (row == face_of + FACES), weight, 0.0).astype(BF16)
    weight_local = lanes_dot(weight_rows[:16], chosen[:AGG])
    weight_ghost = lanes_dot(chosen[AGG:], weight_rows)
    high = weight_ghost.astype(BF16).astype(F32)
    split = jnp.where(iota((4 * GHOST, 128), 1) < FACES, high, weight_ghost - high).astype(BF16)
    for r in range(4):
        message_out[r, :, :WIDTH] = picked[r * GHOST : (r + 1) * GHOST]
        message_out[r, :, WIDTH:] = split[r * GHOST : (r + 1) * GHOST]

    for r in range(4):
        @pl.when(jnp.logical_not(valid[r]))
        def _(r=r):
            message_in[r] = jnp.zeros((GHOST, MESSAGE), BF16)

    near_count = sum(condition.astype(jnp.int32) for condition in valid)
    pl.semaphore_wait(barrier, near_count + is_hub.astype(jnp.int32) * (wide_size - 1))
    ghost_copies = [
        pltpu.make_async_remote_copy(
            src_ref=message_out.at[r],
            dst_ref=message_in.at[r ^ 1],
            send_sem=ghost_send.at[r],
            recv_sem=ghost_recv.at[r ^ 1],
            device_id=neighbours[r],
            device_id_type=MESH,
        )
        for r in range(4)
    ]
    for r in range(4):
        pl.when(valid[r])(ghost_copies[r].start)

    @pl.when(is_hub)
    def _():
        def tell(i, carry):
            step = i // 2 + 1
            peer = lax.rem(w + step + lax.rem(i, 2) * (wide_size - 2 * step), wide_size)
            pl.semaphore_signal(everyone, inc=1, device_id=(g, peer), device_id_type=MESH)
            return carry

        lax.fori_loop(0, wide_size - 1, tell, 0)

    modes_t[...] = modes.T
    loads[6].wait()
    stiff_t[...] = stiff_v[...].T
    for pair in range(MODES // 2):
        two = jnp.concatenate(
            [modes_t[(2 * pair + h) * DOFS : (2 * pair + h + 1) * DOFS] for h in range(2)], axis=1
        )
        near_s[pair] = plain_dot(stiff_t[...], two).astype(BF16)
    for f in range(FACES):
        other_s[f] = plain_dot(modes_t[...], chosen[:AGG, f * AGG : (f + 1) * AGG]).astype(BF16)

    loads[5].wait()
    owner = owner_v[0]
    owned = iota((wide_size, AGG), 0) == owner
    owned_ones = ones_where(owned)
    before = ones_where(iota((AGG, AGG), 0) < iota((AGG, AGG), 1))
    earlier = plain_dot(owned_ones, before)
    rank = jnp.sum(jnp.where(owned, earlier, 0.0), axis=0, keepdims=True).astype(jnp.int32)
    place_s[...] = ones_where(iota((wide_size * CAP, AGG), 0) == owner * CAP + rank)

    def load_near(k):
        def load(m, base):
            return near_s[m // 2, pl.ds(k * DOFS + base, 16), m % 2 * AGG : (m % 2 + 1) * AGG]

        return load

    def load_modes(m, base):
        return modes_t[pl.ds(m * DOFS + base, 16), :]

    zero = jnp.zeros((8, AGG), F32)
    for k in range(1 + FACES):
        sums = list(pair_sums(load_near(k), load_modes)) + [zero] * 4
        for entry in range(0, BLOCK, 8):
            diag_s[k, entry : entry + 8] = row_sums(sums[entry : entry + 8])
    for f in range(FACES):
        sums = pair_sums(load_near(f + 1), lambda n, base, f=f: other_s[f, pl.ds(n * DOFS + base, 16), :])
        for entry in range(BLOCK):
            partial_s[f, entry * 8 : entry * 8 + 8] = sums[entry]

    for r in range(4):
        pl.when(valid[r])(ghost_copies[r ^ 1].wait_recv)
    arrived = jnp.concatenate([message_in[r] for r in range(4)], axis=0)
    ghosts = jnp.concatenate([arrived[:, n * DOFS : (n + 1) * DOFS] for n in range(MODES)], axis=0)
    weight_back = plain_dot(arrived[:, WIDTH:].T[:16], select)
    parts = [zero] * 4
    scale = []
    for f in range(FACES):
        target = jnp.broadcast_to(targets[:, f * AGG : (f + 1) * AGG], (8, AGG)) - AGG
        wanted = [iota((8, AGG), 0) + 8 * group == target for group in range(4 * GHOST // 8)]
        for pair in range(MODES // 2):
            product = plain_dot(ghosts, near_s[pair, (f + 1) * DOFS : (f + 2) * DOFS])
            for half in range(2):
                for n in range(MODES):
                    taken = zero
                    for group, mask in enumerate(wanted):
                        at = n * 4 * GHOST + group * 8
                        taken = jnp.where(mask, product[at : at + 8, half * AGG : (half + 1) * AGG], taken)
                    entry = (2 * pair + half) * MODES + n
                    parts.append(partial_s[f, entry * 8 : entry * 8 + 8] + taken)

    total = []
    for f in range(FACES):
        total.append(
            weight[:, f * AGG : (f + 1) * AGG]
            + weight_local[f : f + 1]
            + (weight_back[f : f + 1] + weight_back[f + FACES : f + FACES + 1])
        )
    diag = diag_s[0]
    for f in range(FACES):
        diag = diag + total[f] * diag_s[f + 1]
    faces = jnp.concatenate([row_sums(parts[e : e + 8]) for e in range(0, FACES * BLOCK + 4, 8)], axis=0)
    factor = jnp.concatenate(
        [jnp.zeros((4, AGG), F32)]
        + [jnp.broadcast_to(-weight[:, f * AGG : (f + 1) * AGG], (BLOCK, AGG)) for f in range(FACES)],
        axis=0,
    )
    faces = faces * factor
    coarse_t = jnp.concatenate([diag[:32], diag[32:] + faces[:8], faces[8:]], axis=0)

    main = coarse_t[:128].astype(BF16)
    early = wide_size // 4

    def main_rows(start, stop):
        first = lanes_dot(place_s[start * CAP : stop * CAP], main).astype(BF16)
        send_s[start:stop, :4] = first.reshape(stop - start, 4, 2, 128)

    last = jnp.concatenate([jnp.where(rank == s, coarse_t[128:], 0.0) for s in range(CAP)], axis=0).astype(BF16)
    last = lanes_dot(owned_ones, last)
    main_rows(0, early)
    send_s[:, 4] = jnp.concatenate([last[:, None], jnp.zeros((wide_size, 1, 128), F32)], axis=1).astype(BF16)

    pl.when(jnp.logical_not(is_hub))(lambda: pl.semaphore_wait(everyone, 1))

    def send_rows(i, carry):
        place = i + (i >= w + 1 - 2 * lax.rem(w, 2)).astype(jnp.int32)
        peer = place + 1 - 2 * lax.rem(place, 2)
        pltpu.make_async_remote_copy(
            src_ref=send_s.at[peer],
            dst_ref=recv_s.at[w],
            send_sem=row_send,
            recv_sem=row_recv.at[w // (wide_size // 2)],
            device_id=(g, peer),
            device_id_type=MESH,
        ).start()
        return carry

    lax.fori_loop(0, early - 1, send_rows, 0)
    main_rows(early, wide_size)
    lax.fori_loop(early - 1, wide_size - 1, send_rows, 0)
    half = wide_size // 2
    pltpu.make_async_copy(send_s.at[w], recv_s.at[w], row_recv.at[w // half]).start()
    for r in range(4):
        pl.when(valid[r])(ghost_copies[r].wait_send)
    columns = half * CAP
    column = iota((half, columns), 1)
    sender = ones_where(column // CAP == iota((half, columns), 0))
    slot = lax.rem(iota((16, columns), 1), CAP)
    for part in range(2):
        rows = recv_s.at[pl.ds(part * half, half)]
        at = slice(part * columns, (part + 1) * columns)
        pltpu.make_async_copy(rows, rows, row_recv.at[part]).wait()
        out_ref[:128, at] = rows[:, :4].reshape(columns, 128).T.astype(F32)
        last = plain_dot(rows[:, 4].astype(F32)[:, 0].T.astype(BF16), sender)
        tail = jnp.zeros((16, columns), F32)
        for s in range(CAP):
            tail = jnp.where(slot == s, last[s * 16 : (s + 1) * 16], tail)
        out_ref[128:, at] = tail
    sent = send_s.at[pl.ds(0, wide_size - 1)]
    pltpu.make_async_copy(sent, sent, row_send).wait()


def solution(mesh):
    grp_size, wide_size = mesh.shape["grp"], mesh.shape["wide"]

    def shards(null_space, node_damage, face_target, face_damage, ghost_lists, agg_owner, stiffness):
        coarse = pl.pallas_call(
            functools.partial(kernel, grp_size, wide_size),
            out_shape=pltpu.VMEM((ROW, wide_size * CAP), F32),
            in_specs=[pl.BlockSpec(memory_space=pltpu.HBM)] * 7,
            out_specs=pl.BlockSpec(memory_space=pltpu.VMEM),
            scratch_shapes=[
                pltpu.VMEM((AGG, WIDTH), BF16),
                pltpu.VMEM((64, AGG), jnp.int32),
                pltpu.VMEM((FACES, 1, AGG), jnp.int32),
                pltpu.VMEM((FACES, 1, AGG), jnp.int32),
                pltpu.VMEM((4, GHOST), jnp.int32),
                pltpu.VMEM((1, 1, AGG), jnp.int32),
                pltpu.VMEM((DOFS, (1 + FACES) * DOFS), BF16),
                pltpu.VMEM((4, GHOST, MESSAGE), BF16),
                pltpu.VMEM((4, GHOST, MESSAGE), BF16),
                pltpu.VMEM((WIDTH, AGG), BF16),
                pltpu.VMEM(((1 + FACES) * DOFS, DOFS), BF16),
                pltpu.VMEM((MODES // 2, (1 + FACES) * DOFS, 2 * AGG), BF16),
                pltpu.VMEM((FACES, WIDTH, AGG), BF16),
                pltpu.VMEM((1 + FACES, BLOCK + 4, AGG), F32),
                pltpu.VMEM((FACES, BLOCK * 8, AGG), F32),
                pltpu.VMEM((wide_size * CAP, AGG), BF16),
                pltpu.VMEM((wide_size, 5, 2, 128), BF16),
                pltpu.VMEM((wide_size, 5, 2, 128), BF16),
                pltpu.SemaphoreType.DMA((7,)),
                pltpu.SemaphoreType.DMA((4,)),
                pltpu.SemaphoreType.DMA((4,)),
                pltpu.SemaphoreType.DMA,
                pltpu.SemaphoreType.DMA((2,)),
                pltpu.SemaphoreType.REGULAR,
            ],
            compiler_params=pltpu.CompilerParams(
                collective_id=0, has_side_effects=True, vmem_limit_bytes=56 * 1024 * 1024
            ),
            cost_estimate=pl.CostEstimate(flops=400_000_000, bytes_accessed=1_000_000, transcendentals=0),
        )(
            null_space[0],
            jnp.transpose(node_damage[0]),
            jnp.transpose(face_target, (2, 0, 1)),
            jnp.transpose(face_damage, (2, 0, 1)),
            ghost_lists[0, 0],
            jnp.transpose(agg_owner, (0, 2, 1)),
            stiffness,
        )
        return coarse[None]

    placed = (
        P("grp", "wide", None),
        P("grp", "wide", None),
        P("grp", "wide", None),
        P("grp", "wide", None),
        P("grp", "wide", None, None),
        P("grp", "wide", None),
        P(),
    )
    return jax.shard_map(
        shards, mesh=mesh, in_specs=placed, out_specs=P("grp", "wide", None), check_vma=False
    )
```
